32 devices in a mesh: ctx: 8 (over z, core), exp: 4 (over y, x).
Axes of the slice: x: 2, y: 2, z: 4, core: 2. Of those that a mesh axis runs over, the one named last changes fastest.
Arguments:
- tokens: bfloat16 [6144, 2048], P(('ctx', 'exp')), may hold values from -6 to 6
- expert_ids: int32 [6144, 1], P(('ctx', 'exp')), may hold values from 0 to 1; in each aligned block of 192 rows (0 to 191, 192 to 383, ...) at most 144 rows name the same one
- damping: bfloat16 [6144], P(('ctx', 'exp')), may hold values from 0 to 0.5, as said below
- in_weight: bfloat16 [4, 2048, 2, 1024], P('exp', 'ctx'), may hold values from -0.125 to 0.125
- out_weight: bfloat16 [4, 1024, 2048], P('exp', None, 'ctx'), may hold values from -0.125 to 0.125
- w_bc: bfloat16 [2048, 256], replicated, may hold values from -0.125 to 0.125
- w_dt: bfloat16 [32, 2048], replicated, may hold values from -0.125 to 0.125
- rate: float32 [32], P('exp'), may hold values from 0 to 3, as said below
- dt_bias: float32 [32], P('exp'), may hold values from -5.5 to -3.5
- d_skip: float32 [32], P('exp'), may hold values from 0.5 to 2
- gain: float32 [2048], P('exp'), may hold values from 0.25 to 1.75
- conv_weight: float32 [4, 2048], P(None, 'exp'), may hold values from -3 to 3
Outputs:
- mixed: bfloat16 [6144, 2048], P(('ctx', 'exp'))
The draws below stay inside these ranges and needn't reach their ends.
Inputs may be any that keep to these rules, and one draw needn't show every extreme that they name: `expert_ids`: among the 192 tokens of one device at most 144 name the same expert, and in every draw some device has an expert named by exactly 144 of its tokens. `damping`: Nonnegative. `rate`: Positive.
All inputs are finite; a program needn't handle non-finite values.
Results may differ from the reference program's by a relative error of at most 0.012.
Values may be sent and summed in bfloat16 or wider, within the bound.
No kernel may reach another device: no remote copies, remote signals or barrier semaphores. Data moves between devices by JAX's collectives and lax.ppermute only.
A program may use at most 128 MiB of HBM per device.

```python
import math
import jax
import jax.numpy as jnp
import numpy as np
from jax import lax

D = 2048
INNER = 2048
HEAD = 64
STATE = 128
CONVW = 4
TOK_DEV = 192
WINDOW_TOKENS = 6144
HEADS = 32
EXPERTS = 2
CAP = 144
N_EXP = 4


pulse_count = 3


def draw_rate(key, part):
    leading_part, trailing_part, third = jax.random.split(jax.random.fold_in(key, 11), 3)
    slow = jnp.exp(jax.random.uniform(leading_part, (HEADS,), jnp.float32, jnp.log(4.0), jnp.log(40.0))) / WINDOW_TOKENS
    quick = jnp.exp(jax.random.uniform(trailing_part, (HEADS,), jnp.float32, jnp.log(1.0), jnp.log(3.0)))
    order = jax.random.permutation(third, HEADS)
    picked = order < HEADS // 2
    return jnp.where(picked, slow, quick).astype(jnp.float32)


def draw_damping(key, part):
    leading_part, trailing_part = jax.random.split(jax.random.fold_in(key, 23), 2)
    slot_positions = jax.random.randint(leading_part, (pulse_count,), 0, WINDOW_TOKENS)
    token_amounts = jax.random.uniform(trailing_part, (pulse_count,), jnp.float32, 0.22, 0.5)
    field = jnp.zeros((WINDOW_TOKENS,), jnp.float32).at[slot_positions].max(token_amounts)
    return field.astype(jnp.bfloat16)


def shard_levels(key, extent, pieces, low, high):
    def one(axis_at, blocks):
        draws = jax.random.uniform(jax.random.fold_in(jax.random.fold_in(key, 6), axis_at), (blocks,), jnp.float32, low / len(pieces), high / len(pieces))
        return jnp.repeat(jnp.exp(draws), extent[axis_at] // blocks).reshape((-1,) + (1,) * (len(extent) - axis_at - 1))

    loudness = one(*pieces[0])
    for cut in pieces[1:]:
        loudness = loudness * one(*cut)
    return loudness


def assign_block(rng, own, number, rows, amount, top, reach, lean):
    ranking = jax.random.permutation(rng, amount)
    heavy_load, common = shares(amount, rows * top, reach, lean, True), shares(amount, rows * top, reach, lean, False)
    places = jnp.arange(amount)

    def named(lengths, turn):
        used = int((lengths > 0).sum())
        fixed = max(1, used // 4)
        shifted = fixed + (places - fixed + turn * (used - fixed)) % max(1, amount - fixed)
        return jnp.zeros((amount,), jnp.int32).at[ranking[jnp.where(places < fixed, places, shifted)]].set(jnp.asarray(lengths, jnp.int32))

    lengths = jnp.where(number % 4 == 0, named(heavy_load, number // 4), named(common, number - number // 4 - 1))
    mixed = jax.random.permutation(jax.random.fold_in(own, 3), amount)
    donor, taker = mixed[0:amount // 2 * 2:2], mixed[1:amount // 2 * 2:2]
    slack = jnp.minimum(lengths[donor] - 1, reach - lengths[taker]) // 2
    slack = jnp.where((donor == ranking[0]) | (taker == ranking[0]) | (lengths[taker] == 0), 0, jnp.maximum(slack, 0))
    shifted = jax.random.randint(jax.random.fold_in(own, 4), (amount // 2,), 0, 1 << 20) % (slack + 1)
    lengths = lengths.at[donor].add(-shifted).at[taker].add(shifted)
    items = jnp.searchsorted(jnp.cumsum(lengths), jnp.arange(rows * top), side="right").astype(jnp.int32)
    listing = items.reshape(top, rows).T
    listing = listing[jax.random.permutation(jax.random.fold_in(own, 1), rows)]
    turn = jax.random.randint(jax.random.fold_in(own, 2), (rows, 1), 0, top)
    return jnp.take_along_axis(listing, (jnp.arange(top)[None, :] + turn) % top, axis=1)


def shares(number_of, total, most, slope, full):
    portions = [(1 << 20) // math.isqrt(rank ** slope) + 1 for rank in range(1, number_of + 1)]
    largest = most if full else min(most, max(-(-total // number_of), total * portions[0] // sum(portions)))
    least = 1 if total - largest >= number_of - 1 else 0
    counts, surplus = [largest] + [least] * (number_of - 1), total - largest - least * (number_of - 1)
    while surplus > 0:
        movable = [i for i in range(1, number_of) if counts[i] < largest] or [i for i in range(1, number_of) if counts[i] < most]
        pool, left = sum([portions[i] for i in movable]), surplus
        for i in movable:
            addition = min(most - counts[i], max(1, left * portions[i] // pool), surplus)
            counts[i] = counts[i] + addition
            surplus = surplus - addition
    return np.array(counts)


def noise(stream_key, extent, scale, most, shards=(), kind=jnp.bfloat16):
    values = scale * jax.random.normal(stream_key, extent, jnp.float32)
    if shards:
        values = values * shard_levels(stream_key, extent, shards, -0.22, 0.18)
    return jnp.clip(values, -most, most).astype(kind)


def setup_inputs(seed: int = 0) -> dict:
    streams_of = jax.random.split(jax.random.key(seed), 13)
    tokens = noise(streams_of[0], (WINDOW_TOKENS, D), 1.0, 6.0, ((0, 32),))
    expert_ids_keys = jax.random.split(jax.random.fold_in(streams_of[1], 1), WINDOW_TOKENS // TOK_DEV)
    expert_ids_turns = jax.random.permutation(jax.random.fold_in(streams_of[1], 3), WINDOW_TOKENS // TOK_DEV)
    expert_ids = jax.vmap(lambda own, number: assign_block(jax.random.fold_in(streams_of[1], 2), own, number, TOK_DEV, EXPERTS, 1, CAP, 2))(expert_ids_keys, expert_ids_turns).reshape((WINDOW_TOKENS, 1))
    damping = draw_damping(jax.random.fold_in(streams_of[12], 71), 0)
    in_weight = noise(streams_of[3], (2 * EXPERTS, D, 2, INNER // 2), D ** -0.5, 0.125, ((0, 4), (1, 8)))
    out_weight = noise(streams_of[4], (2 * EXPERTS, INNER // 2, D), INNER ** -0.5, 0.125, ((0, 4), (2, 8)))
    w_bc = noise(streams_of[5], (D, 2 * STATE), D ** -0.5, 0.125)
    w_dt = noise(streams_of[6], (HEADS, D), D ** -0.5, 0.125)
    rate = draw_rate(jax.random.fold_in(streams_of[12], 71), 0)
    dt_bias = jnp.clip(-5.5 + 2.0 * jax.random.uniform(streams_of[8], (HEADS,), jnp.float32) ** shard_levels(streams_of[8], (HEADS,), ((0, 4),), -0.2, 0.2), -5.5, -3.5)
    d_skip = jnp.clip(0.5 + 1.5 * jax.random.uniform(streams_of[9], (HEADS,), jnp.float32) ** shard_levels(streams_of[9], (HEADS,), ((0, 4),), -0.2, 0.2), 0.5, 2.0)
    gain = jnp.clip(1.0 + 0.15 * jax.random.normal(streams_of[10], (INNER,), jnp.float32), 0.25, 1.75)
    conv_weight = noise(streams_of[11], (CONVW, INNER), CONVW ** -0.5, 3.0, ((1, 4),), jnp.float32)
    return {"tokens": tokens, "expert_ids": expert_ids, "damping": damping, "in_weight": in_weight, "out_weight": out_weight, "w_bc": w_bc, "w_dt": w_dt, "rate": rate, "dt_bias": dt_bias, "d_skip": d_skip, "gain": gain, "conv_weight": conv_weight}


block_len = 256
highest = lax.Precision.HIGHEST

def routing(expert_ids):
    chosen = expert_ids[:, 0].astype(jnp.int32)
    grouped = chosen.reshape(-1, TOK_DEV)
    onehot = (grouped[:, :, None] == jnp.arange(EXPERTS, dtype=jnp.int32)[None, None, :]).astype(jnp.int32)
    before = jnp.cumsum(onehot, axis=1) - onehot
    position = lax.optimization_barrier(jnp.sum(before * onehot, axis=2))
    offset = jnp.arange(grouped.shape[0], dtype=jnp.int32)[:, None] * CAP
    return (chosen, (offset + position).reshape(-1).astype(jnp.int32))

def per_expert(values, chosen, slot_positions, project, width):
    row_total = WINDOW_TOKENS // TOK_DEV * CAP

    def visit(total, expert):
        target = jnp.where(chosen == expert, slot_positions, row_total).astype(jnp.int32)
        buffer = jnp.zeros((row_total, values.shape[1]), values.dtype).at[target].set(values, mode='drop')
        result = project(expert, buffer)
        taken = result[slot_positions]
        return (jnp.where((chosen == expert)[:, None], taken, total), None)
    start = jnp.zeros((values.shape[0], width), jnp.bfloat16)
    total, _ = lax.scan(visit, start, jnp.arange(EXPERTS, dtype=jnp.int32))
    return total

def scan_heads(inputs, steps, decays, keys, queries, d_skip):
    count = WINDOW_TOKENS // block_len
    block = block_len
    lower = (jnp.arange(block)[:, None] >= jnp.arange(block)[None, :])[:, :, None]

    def advance(state, item):
        values, sizes, logs, keyrows, queryrows = item
        climb = jnp.cumsum(logs, axis=0)
        gram = jnp.dot(queryrows, keyrows.T, precision=highest)
        spread = jnp.where(lower, jnp.exp(jnp.where(lower, climb[:, None, :] - climb[None, :, :], 0.0)), 0.0)
        scaled = sizes[:, :, None] * values
        inside = jnp.einsum('ijh,ij,jhd->ihd', spread, gram, scaled, precision=highest)
        carried = jnp.exp(climb)[:, :, None] * jnp.einsum('in,hdn->ihd', queryrows, state, precision=highest)
        ending = jnp.exp(climb[-1][None, :] - climb)
        fresh = jnp.einsum('jh,jhd,jn->hdn', ending, scaled, keyrows, precision=highest)
        state = jnp.exp(climb[-1])[:, None, None] * state + fresh
        return (state, inside + carried + d_skip[None, :, None] * values)
    items = (inputs.reshape(count, block, HEADS, HEAD), steps.reshape(count, block, HEADS), decays.reshape(count, block, HEADS), keys.reshape(count, block, STATE), queries.reshape(count, block, STATE))
    _, output = lax.scan(advance, jnp.zeros((HEADS, HEAD, STATE), jnp.float32), items)
    return output.reshape(WINDOW_TOKENS, HEADS, HEAD)

def reference(tokens, expert_ids, damping, in_weight, out_weight, w_bc, w_dt, rate, dt_bias, d_skip, gain, conv_weight):
    chosen, slot_positions = routing(expert_ids)
    half = INNER // 2
    piece = INNER // (2 * N_EXP)

    def project_in(expert, buffer):
        both = jnp.concatenate([in_weight[2 * expert].reshape(D, INNER), in_weight[2 * expert + 1].reshape(D, INNER)], axis=1)
        return jnp.dot(buffer, both, preferred_element_type=jnp.float32).astype(jnp.bfloat16)
    projected = per_expert(tokens, chosen, slot_positions, project_in, 2 * INNER)
    projected = lax.optimization_barrier(projected)
    grid = projected.reshape(WINDOW_TOKENS, 2, 2, N_EXP, piece)
    inner_x = grid[:, :, 0].transpose(0, 2, 1, 3).reshape(WINDOW_TOKENS, INNER)
    inner_z = grid[:, :, 1].transpose(0, 2, 1, 3).reshape(WINDOW_TOKENS, INNER)
    shared = lax.optimization_barrier(jnp.dot(tokens, w_bc, preferred_element_type=jnp.float32).astype(jnp.bfloat16))
    dt_raw = lax.optimization_barrier(jnp.dot(tokens, w_dt.T, preferred_element_type=jnp.float32).astype(jnp.bfloat16))
    padded = jnp.concatenate([jnp.zeros((CONVW - 1, INNER), inner_x.dtype), inner_x], axis=0).astype(jnp.float32)
    convolved = jnp.zeros((WINDOW_TOKENS, INNER), jnp.float32)
    for tap in range(CONVW):
        convolved = convolved + conv_weight[tap][None, :] * padded[tap:tap + WINDOW_TOKENS]
    inputs = jax.nn.silu(convolved)
    steps = jax.nn.softplus(dt_raw.astype(jnp.float32) + dt_bias[None, :])
    decays = -(rate[None, :] * steps + damping.astype(jnp.float32)[:, None])
    keys = shared[:, :STATE].astype(jnp.float32)
    queries = shared[:, STATE:].astype(jnp.float32)
    scan_output = scan_heads(inputs, steps, decays, keys, queries, d_skip)
    gated = scan_output * jax.nn.silu(inner_z.astype(jnp.float32).reshape(WINDOW_TOKENS, HEADS, HEAD))
    scale = lax.rsqrt(lax.optimization_barrier(jnp.mean(gated * gated, axis=2, keepdims=True)) + 1e-05)
    normed = (gated * scale * gain.reshape(HEADS, HEAD)[None]).astype(jnp.bfloat16).reshape(WINDOW_TOKENS, INNER)
    split = normed.reshape(WINDOW_TOKENS, N_EXP, 2, piece)
    sorted_rows = jnp.concatenate([split[:, :, 0].reshape(WINDOW_TOKENS, half), split[:, :, 1].reshape(WINDOW_TOKENS, half)], axis=1)

    def project_out(expert, buffer):
        leading_part = jnp.dot(buffer[:, :half], out_weight[2 * expert], preferred_element_type=jnp.float32).astype(jnp.bfloat16)
        trailing_part = jnp.dot(buffer[:, half:], out_weight[2 * expert + 1], preferred_element_type=jnp.float32).astype(jnp.bfloat16)
        leading_part = lax.optimization_barrier(leading_part).astype(jnp.float32)
        trailing_part = lax.optimization_barrier(trailing_part).astype(jnp.float32)
        return (leading_part + trailing_part).astype(jnp.bfloat16)
    return per_expert(sorted_rows, chosen, slot_positions, project_out, D)
```

```python
import functools

import jax
import jax.numpy as jnp
from jax import lax
from jax.experimental import pallas as pl
from jax.experimental.pallas import tpu as pltpu
from jax.sharding import PartitionSpec as P

both = ("ctx", "exp")
extra = 128
halo = 16
dt_lane, reach_lane = 16, 32
highest = lax.Precision.HIGHEST
f32, bf16 = jnp.float32, jnp.bfloat16


def params(mib):
    return pltpu.CompilerParams(vmem_limit_bytes=mib << 20)


def vmem(*shape):
    return pl.BlockSpec(shape, lambda *_: (0,) * len(shape), pipeline_mode=pl.Buffered(1))


def shift(array, move):
    groups = lax.axis_size("exp")
    pairs = []
    for c in range(lax.axis_size("ctx")):
        for e in range(groups):
            to = move(c // 2, c % 2, e)
            if to is not None:
                pairs.append((c * groups + e, (2 * to[0] + to[1]) * groups + to[2]))
    return lax.ppermute(array, both, pairs)


def line_gather(own, depth):
    if depth == 1:
        return [own], []
    first = shift(own, lambda z, k, e: ((z + 1) % depth, k, e))
    last = shift(own, lambda z, k, e: ((z - 1) % depth, k, e)) if depth > 2 else None
    ups, downs = [], []
    up, down = first, last
    for s in range(2, depth - 1):
        up = shift(up, lambda z, k, e: (z + 1, k, e) if s - 1 <= z < depth - 1 else None)
        down = shift(down, lambda z, k, e: (z - 1, k, e) if 0 < z <= depth - s else None)
        ups.append(up)
        downs.append(down)
    middle = [(ups[s - 2], downs[depth - s - 2]) for s in range(2, depth - 1)]
    return [own, first] + ([last] if depth > 2 else []), middle


def maps_kernel(heads, width, x_ref, w_ref, bias_ref, rate_ref, maps_ref, cols_ref, rows_ref, total):
    length = x_ref.shape[0]

    @pl.when(pl.program_id(0) == 0)
    def _():
        total[...] = jnp.zeros_like(total)

    found = jnp.dot(x_ref[:, :width], w_ref[...], preferred_element_type=f32).astype(bf16)
    state2 = maps_ref.shape[1]
    maps_ref[...] = found[:, :state2]
    raw = found[:, state2:].astype(f32) + bias_ref[...]
    steps = jnp.maximum(raw, 0.0) + jnp.log1p(jnp.exp(-jnp.abs(raw)))
    damping = x_ref[:, width : width + extra].astype(f32)[:, 1:2]
    logs = -(rate_ref[...] * steps + damping)
    row = lax.broadcasted_iota(jnp.int32, (length, length), 0)
    col = lax.broadcasted_iota(jnp.int32, (length, length), 1)
    lower = (row >= col).astype(f32)
    climb = jnp.dot(lower, logs, precision=highest, preferred_element_type=f32)
    lane = lax.broadcasted_iota(jnp.int32, climb.shape, 1)
    reach = climb + total[...]
    packed = jnp.where(lane < dt_lane, climb, jnp.where(lane < reach_lane, steps, reach))
    cols_ref[...] = packed
    rows_ref[...] = jnp.transpose(packed)[: rows_ref.shape[0]]
    total[...] = reach[length - 1 : length]


def maps(tokens, w_maps, bias, rate, heads, state2, length):
    count, width = tokens.shape[0], w_maps.shape[0]
    return pl.pallas_call(
        functools.partial(maps_kernel, heads, width),
        grid=(count // length,),
        in_specs=[
            pl.BlockSpec((length, tokens.shape[1]), lambda b: (b, 0)),
            vmem(*w_maps.shape),
            vmem(1, 128),
            vmem(1, 128),
        ],
        out_specs=[
            pl.BlockSpec((length, state2), lambda b: (b, 0)),
            pl.BlockSpec((length, 128), lambda b: (b, 0)),
            pl.BlockSpec((reach_lane, length), lambda b: (0, b)),
        ],
        out_shape=[
            jax.ShapeDtypeStruct((count, state2), bf16),
            jax.ShapeDtypeStruct((count, 128), f32),
            jax.ShapeDtypeStruct((reach_lane, count), f32),
        ],
        scratch_shapes=[pltpu.VMEM((1, 128), f32)],
        compiler_params=params(32),
        name="maps",
    )(tokens, w_maps, bias, rate)


def scan_kernel(
    first_head, head, experts, depth, width, near, middle, pos_ref, x_ref, edge_ref, *refs
):
    slots = refs[: near + 2 * middle]
    maps_ref, cols_ref, rows_ref, taps_ref, skip_ref = refs[near + 2 * middle :][:5]
    y_ref, gate_ref, final_ref, whole, seen, state = refs[near + 2 * middle + 5 :]
    length, channels = y_ref.shape
    taps = taps_ref.shape[0]
    width_state = maps_ref.shape[1] // 2
    step, z = pl.program_id(0), pos_ref[0]
    depth_rows = width // depth

    def place(ref, distance):
        rows = pl.ds(pl.multiple_of(lax.rem(z - distance + depth, depth) * depth_rows, 128), depth_rows)
        for e in range(experts):
            whole[e, rows, :] = ref[e * depth_rows : (e + 1) * depth_rows, :]

    def project(tokens):
        chosen = tokens[:, width : width + extra].astype(f32)[:, 0:1]
        total = jnp.dot(tokens[:, :width], whole[0], preferred_element_type=f32)
        for e in range(1, experts):
            other = jnp.dot(tokens[:, :width], whole[e], preferred_element_type=f32)
            total = jnp.where(chosen == e, other, total)
        total = total.astype(bf16)
        return total[:, :channels], total[:, channels:]

    @pl.when(step == 0)
    def _():
        for at, distance in zip(range(near), (0, 1, depth - 1)):
            place(slots[at], distance)
        for at in range(middle):
            distance = at + 2

            @pl.when(z >= distance)
            def _():
                place(slots[near + 2 * at], distance)

            @pl.when(z < distance)
            def _():
                place(slots[near + 2 * at + 1], distance)

        before, _ = project(edge_ref[...])
        seen[0:8, :] = before[halo - 8 :].astype(f32)
        state[...] = jnp.zeros_like(state)

    inner, gate = project(x_ref[...])
    gate_ref[...] = gate
    seen[8:, :] = inner.astype(f32)
    mixed = jnp.zeros((length, channels), f32)
    for tap in range(taps):
        mixed = mixed + taps_ref[tap : tap + 1, :] * seen[pl.ds(8 - (taps - 1) + tap, length), :]
    seen[0:8, :] = seen[pl.ds(length, 8), :]
    values = mixed / (1.0 + jnp.exp(-mixed))

    keys, queries = maps_ref[:, :width_state], maps_ref[:, width_state:]
    gram = lax.dot_general(queries, keys, (((1,), (1,)), ((), ())), preferred_element_type=f32)
    row = lax.broadcasted_iota(jnp.int32, (length, length), 0)
    col = lax.broadcasted_iota(jnp.int32, (length, length), 1)
    lower = row >= col
    gram = jnp.where(lower, gram, 0.0)
    lane = lax.broadcasted_iota(jnp.int32, (1, channels), 1)
    rounded = values.astype(bf16)
    inside, growth, ends, decay = [], 0.0, 0.0, 0.0
    reached = 0.0
    for j in range(channels // head):
        at = first_head + j
        mine = lane // head == j
        climb, size = cols_ref[:, at : at + 1], cols_ref[:, dt_lane + at : dt_lane + at + 1]
        climb_row, size_row = rows_ref[at : at + 1, :], rows_ref[dt_lane + at : dt_lane + at + 1, :]
        spread = jnp.exp(jnp.where(lower, climb - climb_row, 0.0)) * gram * size_row
        inside.append(
            jnp.dot(
                spread.astype(bf16), rounded[:, j * head : (j + 1) * head], preferred_element_type=f32
            )
        )
        last = climb[length - 1 : length]
        growth = jnp.where(mine, jnp.exp(climb), growth)
        ends = jnp.where(mine, jnp.exp(last - climb) * size, ends)
        decay = jnp.where(mine, jnp.exp(last), decay)
        reach = cols_ref[length - 1 : length, reach_lane + at : reach_lane + at + 1]
        reached = jnp.where(mine, reach, reached)
    inside = inside[0] if len(inside) == 1 else jnp.concatenate(inside, axis=1)
    carried = jnp.dot(queries, state[...].astype(bf16), preferred_element_type=f32)
    y_ref[...] = inside + growth * carried + skip_ref[...] * values
    fresh = lax.dot_general(
        keys, (ends * values).astype(bf16), (((0,), (0,)), ((), ())), preferred_element_type=f32
    )
    state[...] = decay * state[...] + fresh

    @pl.when(step == pl.num_programs(0) - 1)
    def _():
        final_ref[:width_state, :] = state[...]
        final_ref[width_state:, :] = jnp.broadcast_to(reached, (8, channels))


def scan(z, tokens, edge, slots, middle, found, taps, skip, first_head, head, experts, depth, width, length):
    maps_all, cols, rows = found
    count, channels = tokens.shape[0], taps.shape[1]
    width_state = maps_all.shape[1] // 2
    flat = list(slots) + [part for pair in middle for part in pair]
    block = lambda *shape: pl.BlockSpec(shape, lambda b, _: (b, 0))
    return pl.pallas_call(
        functools.partial(
            scan_kernel, first_head, head, experts, depth, width, len(slots), len(middle)
        ),
        grid_spec=pltpu.PrefetchScalarGridSpec(
            num_scalar_prefetch=1,
            grid=(count // length,),
            in_specs=[block(length, tokens.shape[1]), vmem(*edge.shape)]
            + [vmem(*part.shape) for part in flat]
            + [
                block(length, maps_all.shape[1]),
                block(length, 128),
                pl.BlockSpec((rows.shape[0], length), lambda b, _: (0, b)),
                vmem(*taps.shape),
                vmem(*skip.shape),
            ],
            out_specs=[
                block(length, channels),
                block(length, channels),
                pl.BlockSpec((width_state + 8, channels), lambda b, _: (0, 0)),
            ],
            scratch_shapes=[
                pltpu.VMEM((experts, width, 2 * channels), bf16),
                pltpu.VMEM((8 + length, channels), f32),
                pltpu.VMEM((width_state, channels), f32),
            ],
        ),
        out_shape=[
            jax.ShapeDtypeStruct((count, channels), f32),
            jax.ShapeDtypeStruct((count, channels), bf16),
            jax.ShapeDtypeStruct((width_state + 8, channels), f32),
        ],
        compiler_params=params(48),
        name="scan",
    )(z, tokens, edge, *flat, maps_all, cols, rows, taps, skip)


def norm_kernel(chunks, before, head, heads, pos_ref, maps_ref, cols_ref, gain_ref, *refs):
    ys, gates = refs[:chunks], refs[chunks : 2 * chunks]
    finals = refs[2 * chunks : 2 * chunks + chunks * before]
    out_ref, entering = refs[2 * chunks + chunks * before :]
    width_state = maps_ref.shape[1] // 2
    channels = out_ref.shape[1]
    each = channels // chunks

    @pl.when(pl.program_id(0) == 0)
    def _():
        for q in range(chunks):
            total = jnp.zeros((width_state, each), f32)
            logs = jnp.zeros((1, each), f32)
            for s in range(before):
                ref = finals[q * before + s]
                total = total + jnp.exp(logs) * ref[:width_state, :]
                logs = logs + ref[width_state : width_state + 1, :]
            entering[:, q * each : (q + 1) * each] = total.astype(bf16)

    lane = lax.broadcasted_iota(jnp.int32, (1, channels), 1)
    growth = 0.0
    for j in range(heads):
        reach = cols_ref[:, reach_lane + j : reach_lane + j + 1]
        growth = jnp.where(lane // head == j, jnp.exp(reach), growth)
    queries = maps_ref[:, width_state:]
    carried = growth * jnp.dot(queries, entering[...], preferred_element_type=f32)
    join = lambda parts: parts[0][...] if chunks == 1 else jnp.concatenate([p[...] for p in parts], axis=1)
    gate = join(gates).astype(f32)
    gated = (join(ys) + carried) * (gate / (1.0 + jnp.exp(-gate)))
    row = lax.broadcasted_iota(jnp.int32, (channels, channels), 0) // head
    col = lax.broadcasted_iota(jnp.int32, (channels, channels), 1) // head
    same = (row == col).astype(f32)
    square = jnp.dot(gated * gated, same, precision=highest, preferred_element_type=f32) * (1.0 / head)
    out_ref[...] = (gated * lax.rsqrt(square + 1e-05) * gain_ref[...]).astype(bf16)


def norm(part, found, gain, ys, gates, finals, head, length):
    maps_all, cols, _ = found
    count, channels = maps_all.shape[0] // 2, gain.shape[1]
    chunks, before = len(ys), len(finals[0])
    steps = count // length
    block = lambda *shape: pl.BlockSpec(shape, lambda b, at: (at[0] * steps + b, 0))
    flat = [array for group in finals for array in group]
    return pl.pallas_call(
        functools.partial(norm_kernel, chunks, before, head, channels // head),
        grid_spec=pltpu.PrefetchScalarGridSpec(
            num_scalar_prefetch=1,
            grid=(steps,),
            in_specs=[block(length, maps_all.shape[1]), block(length, 128), vmem(*gain.shape)]
            + [block(length, channels // chunks)] * (2 * chunks)
            + [vmem(*array.shape) for array in flat],
            out_specs=pl.BlockSpec((length, channels), lambda b, _: (b, 0)),
            scratch_shapes=[pltpu.VMEM((maps_all.shape[1] // 2, channels), bf16)],
        ),
        out_shape=jax.ShapeDtypeStruct((count, channels), bf16),
        compiler_params=params(32),
        name="norm",
    )(part, maps_all, cols, gain, *ys, *gates, *flat)


def out_kernel(experts, groups, pos_ref, ids_ref, mine_ref, other_ref, w_mine_ref, w_other_ref, *outs):
    group, width = pos_ref[0], mine_ref.shape[0] // groups
    chunk = w_mine_ref.shape[2]
    for s in range(groups):
        rows = pl.ds(pl.multiple_of(jnp.bitwise_xor(group, s) * width, 64), width)
        chosen = ids_ref[rows, :].astype(f32)[:, 0:1]
        mine, other = mine_ref[rows, :], other_ref[rows, :]
        zero = jnp.zeros_like(mine)
        for k in range(2):
            total = jnp.zeros((width, chunk), f32)
            for e in range(experts):
                total += jnp.dot(jnp.where(chosen == e, mine, zero), w_mine_ref[2 * e + k], preferred_element_type=f32)
                total += jnp.dot(jnp.where(chosen == e, other, zero), w_other_ref[2 * e + k], preferred_element_type=f32)
            outs[s][:, k * chunk : (k + 1) * chunk] = total.astype(bf16)


def project_out(group, ids, mine, other, w_mine, w_other, groups):
    experts, chunk = w_mine.shape[0] // 2, w_mine.shape[2]
    rows = mine.shape[0] // groups
    whole = pl.BlockSpec(memory_space=pltpu.VMEM)
    return pl.pallas_call(
        functools.partial(out_kernel, experts, groups),
        in_specs=[pl.BlockSpec(memory_space=pltpu.SMEM)] + [whole] * 5,
        out_specs=[whole] * groups,
        out_shape=[jax.ShapeDtypeStruct((rows, 2 * chunk), bf16)] * groups,
        compiler_params=params(48),
        name="project_out",
    )(group, ids, mine, other, w_mine, w_other)


def sum_kernel(depth, groups, pos_ref, *refs):
    out_ref = refs[-1]
    for s in range(depth):
        parts = refs[s * groups : (s + 1) * groups]
        total = parts[0][...].astype(f32)
        for part in parts[1:]:
            total = total + part[...].astype(f32)
        wide = total.shape[1]
        at = pl.multiple_of(lax.rem(pos_ref[0] - s + depth, depth) * wide, 128)
        out_ref[:, pl.ds(at, wide)] = total.astype(bf16)


def add_up(z, parts, depth, groups):
    rows, wide = parts[0].shape
    whole = pl.BlockSpec(memory_space=pltpu.VMEM)
    return pl.pallas_call(
        functools.partial(sum_kernel, depth, groups),
        in_specs=[pl.BlockSpec(memory_space=pltpu.SMEM)] + [whole] * len(parts),
        out_specs=whole,
        out_shape=jax.ShapeDtypeStruct((rows, depth * wide), bf16),
        compiler_params=params(48),
        name="add_up",
    )(z, *parts)


def spread_pieces(piece_of, groups):
    index = 2 * (lax.axis_index("exp") // 2) + lax.axis_index("ctx") % 2
    return [
        shift(
            piece_of(jnp.bitwise_xor(index, r)),
            lambda z, k, e: (z, e % 2, (2 * (e // 2) + k) ^ r),
        )
        for r in range(groups)
    ]


def arrange(blocks, group):
    stacked = jnp.zeros((len(blocks),) + blocks[0].shape, blocks[0].dtype)
    for r, block in enumerate(blocks):
        stacked = lax.dynamic_update_index_in_dim(stacked, block, jnp.bitwise_xor(group, r), 0)
    return stacked


def on_device(
    tokens, expert_ids, damping, in_weight, out_weight, w_bc, w_dt, rate, dt_bias, d_skip, gain, conv_weight
):
    groups, parts = lax.axis_size("exp"), lax.axis_size("ctx")
    depth, experts = parts // 2, groups // 2
    group, core, z = lax.axis_index("exp"), lax.axis_index("ctx") % 2, lax.axis_index("ctx") // 2
    rows, width = tokens.shape
    half = in_weight.shape[3]
    piece = half // groups
    heads = rate.shape[0] // 2
    head = piece // heads
    chunks = 2 if piece % 256 == 0 else 1
    channels = piece // chunks
    count = 2 * groups * rows
    length = 256 if count % 512 == 0 else 128
    scalar = lambda v: jnp.reshape(v, (1,)).astype(jnp.int32)
    z_at, group_at = scalar(z), scalar(group)
    depth_weight = in_weight.shape[1]

    flat = in_weight[0].reshape(depth_weight, 2 * half)
    in_slots = []
    for q in range(chunks):

        def piece_of(p):
            at = p * piece + q * channels
            return jnp.concatenate(
                [lax.dynamic_slice(flat, (0, j * half + at), (depth_weight, channels)) for j in range(2)],
                axis=1,
            )

        shard = arrange(spread_pieces(piece_of, groups), group)
        shard = shard.reshape(groups * depth_weight, 2 * channels)
        in_slots.append(line_gather(shard, depth))

    added = jnp.concatenate(
        [expert_ids.astype(bf16), damping[:, None], jnp.zeros((rows, extra - 2), bf16)], axis=1
    )
    wide = jnp.concatenate([tokens, added], axis=1)
    own = [wide] + [shift(wide, lambda z, k, e: (z, k, e ^ s)) for s in range(1, groups)]
    swapped = [shift(block, lambda z, k, e: (z, 1 - k, e)) for block in own]
    plane = jnp.zeros((count, width + extra), bf16)
    for where, blocks in ((core, own), (1 - core, swapped)):
        for s, block in enumerate(blocks):
            at = (where * groups + jnp.bitwise_xor(group, s)) * rows
            plane = lax.dynamic_update_slice(plane, block, (at, 0))
    edge = shift(plane[count - halo :], lambda z, k, e: (z + 1, k, e) if z + 1 < depth else None)

    local = lambda vector: lax.dynamic_slice_in_dim(vector, core * heads, heads, 0)
    lanes = lambda vector: jnp.concatenate(
        [jnp.pad(local(vector), (0, dt_lane - heads))] * (128 // dt_lane)
    )[None, :]
    picked = lax.dynamic_slice_in_dim(w_dt, (2 * group + core) * heads, heads, 0)
    picked = jnp.concatenate([jnp.pad(picked, ((0, dt_lane - heads), (0, 0)))] * (128 // dt_lane), axis=0)
    w_maps = jnp.concatenate([w_bc, picked.T], axis=1)
    found = maps(plane, w_maps, lanes(dt_bias), lanes(rate), heads, w_bc.shape[1], length)

    half_taps = lax.dynamic_slice_in_dim(conv_weight, core * piece, piece, 1)
    half_gain = lax.dynamic_slice_in_dim(gain, core * piece, piece, 0)[None, :]
    half_skip = jnp.repeat(local(d_skip), head)[None, :]
    ys, gates, finals = [], [], []
    for q in range(chunks):
        span = slice(q * channels, (q + 1) * channels)
        y, gate, final = scan(
            z_at, plane, edge, *in_slots[q], found, half_taps[:, span], half_skip[:, span],
            q * channels // head, head, experts, depth, width, length,
        )
        ys.append(y)
        gates.append(gate)
        finals.append(
            [
                shift(final, lambda z, k, e: (z + s, k, e) if z + s < depth else None)
                for s in range(1, depth)
            ]
        )

    out_flat = out_weight[0]
    out_blocks = spread_pieces(
        lambda p: lax.dynamic_slice_in_dim(out_flat, p * piece, piece, 0), groups
    )
    near, middle = line_gather(arrange(out_blocks, group), depth)
    ordered = near[:2] + [
        jnp.where(z >= s + 2, up, down) for s, (up, down) in enumerate(middle)
    ] + near[2:]
    other_half = [shift(array, lambda z, k, e: (z, 1 - k, e)) for array in ordered]

    theirs = norm(scalar(1 - core), found, half_gain, ys, gates, finals, head, length)
    other = shift(theirs, lambda z, k, e: (z, 1 - k, e))
    mine = norm(scalar(core), found, half_gain, ys, gates, finals, head, length)

    ids = lax.dynamic_slice(plane, (core * groups * rows, width), (groups * rows, extra))
    blocks = []
    for s in range(depth):
        results = project_out(group_at, ids, mine, other, ordered[s], other_half[s], groups)
        blocks += [results[0]] + [
            shift(results[r], lambda z, k, e: (z, k, e ^ r)) for r in range(1, groups)
        ]
    return add_up(z_at, blocks, depth, groups)


def solution(mesh):
    placed = (
        P(("ctx", "exp"), None),
        P(("ctx", "exp"), None),
        P(("ctx", "exp")),
        P("exp", "ctx", None, None),
        P("exp", None, "ctx"),
        P(),
        P(),
        P("exp"),
        P("exp"),
        P("exp"),
        P("exp"),
        P(None, "exp"),
    )
    return jax.shard_map(
        on_device, mesh=mesh, in_specs=placed, out_specs=P(("ctx", "exp"), None), check_vma=False
    )
```

```python
import functools

import jax
import jax.numpy as jnp
from jax import lax
from jax.experimental import pallas as pl
from jax.experimental.pallas import tpu as pltpu
from jax.sharding import PartitionSpec as P

both = ("ctx", "exp")
extra = 128
halo = 16
dt_lane, reach_lane = 16, 32
highest = lax.Precision.HIGHEST
f32, bf16 = jnp.float32, jnp.bfloat16


def params(mib):
    return pltpu.CompilerParams(vmem_limit_bytes=mib << 20)


def vmem(*shape):
    return pl.BlockSpec(shape, lambda *_: (0,) * len(shape), pipeline_mode=pl.Buffered(1))


def shift(array, move):
    groups = lax.axis_size("exp")
    pairs = []
    for c in range(lax.axis_size("ctx")):
        for e in range(groups):
            to = move(c // 2, c % 2, e)
            if to is not None:
                pairs.append((c * groups + e, (2 * to[0] + to[1]) * groups + to[2]))
    return lax.ppermute(array, both, pairs)


def line_near(own, depth):
    return (
        shift(own, lambda z, k, e: ((z + 1) % depth, k, e)),
        shift(own, lambda z, k, e: ((z - 1) % depth, k, e)),
    )


def step_up(array, s, depth):
    return shift(array, lambda z, k, e: (z + 1, k, e) if s - 1 <= z < depth - 1 else None)


def step_down(array, s, depth):
    return shift(array, lambda z, k, e: (z - 1, k, e) if 0 < z <= depth - s else None)


def line_far(near, depth):
    ups, downs = [], []
    up, down = near
    for s in range(2, depth - 1):
        up, down = step_up(up, s, depth), step_down(down, s, depth)
        ups.append(up)
        downs.append(down)
    return paired(ups, downs)


def paired(ups, downs):
    return list(zip(ups, downs[::-1]))


def maps_kernel(heads, width, x_ref, w_ref, bias_ref, rate_ref, maps_ref, cols_ref, rows_ref, total):
    length = x_ref.shape[0]

    @pl.when(pl.program_id(0) == 0)
    def _():
        total[...] = jnp.zeros_like(total)

    found = jnp.dot(x_ref[:, :width], w_ref[...], preferred_element_type=f32).astype(bf16)
    state2 = maps_ref.shape[1]
    maps_ref[...] = found[:, :state2]
    raw = found[:, state2:].astype(f32) + bias_ref[...]
    steps = jnp.maximum(raw, 0.0) + jnp.log1p(jnp.exp(-jnp.abs(raw)))
    damping = x_ref[:, width : width + extra].astype(f32)[:, 1:2]
    logs = -(rate_ref[...] * steps + damping)
    row = lax.broadcasted_iota(jnp.int32, (length, length), 0)
    col = lax.broadcasted_iota(jnp.int32, (length, length), 1)
    lower = (row >= col).astype(f32)
    climb = jnp.dot(lower, logs, precision=highest, preferred_element_type=f32)
    lane = lax.broadcasted_iota(jnp.int32, climb.shape, 1)
    reach = climb + total[...]
    packed = jnp.where(lane < dt_lane, climb, jnp.where(lane < reach_lane, steps, reach))
    cols_ref[...] = packed
    rows_ref[...] = jnp.transpose(packed)[: rows_ref.shape[0]]
    total[...] = reach[length - 1 : length]


def maps(tokens, w_maps, bias, rate, heads, state2, length):
    count, width = tokens.shape[0], w_maps.shape[0]
    return pl.pallas_call(
        functools.partial(maps_kernel, heads, width),
        grid=(count // length,),
        in_specs=[
            pl.BlockSpec((length, tokens.shape[1]), lambda b: (b, 0)),
            vmem(*w_maps.shape),
            vmem(1, 128),
            vmem(1, 128),
        ],
        out_specs=[
            pl.BlockSpec((length, state2), lambda b: (b, 0)),
            pl.BlockSpec((length, 128), lambda b: (b, 0)),
            pl.BlockSpec((reach_lane, length), lambda b: (0, b)),
        ],
        out_shape=[
            jax.ShapeDtypeStruct((count, state2), bf16),
            jax.ShapeDtypeStruct((count, 128), f32),
            jax.ShapeDtypeStruct((reach_lane, count), f32),
        ],
        scratch_shapes=[pltpu.VMEM((1, 128), f32)],
        compiler_params=params(32),
        name="maps",
    )(tokens, w_maps, bias, rate)


def scan_kernel(
    first_head, head, experts, depth, width, near, middle, pos_ref, x_ref, edge_ref, *refs
):
    slots = refs[: near + 2 * middle]
    maps_ref, cols_ref, rows_ref, taps_ref, skip_ref = refs[near + 2 * middle :][:5]
    earlier = refs[near + 2 * middle + 5 : -6]
    y_ref, gate_ref, final_ref, whole, seen, state = refs[-6:]
    length, channels = y_ref.shape
    taps = taps_ref.shape[0]
    width_state = maps_ref.shape[1] // 2
    step, z = pl.program_id(0), pos_ref[0]
    depth_rows = width // depth

    def place(ref, distance):
        rows = pl.ds(pl.multiple_of(lax.rem(z - distance + depth, depth) * depth_rows, 128), depth_rows)
        for e in range(experts):
            whole[e, rows, :] = ref[e * depth_rows : (e + 1) * depth_rows, :]

    def project(tokens):
        chosen = tokens[:, width : width + extra].astype(f32)[:, 0:1]
        total = jnp.dot(tokens[:, :width], whole[0], preferred_element_type=f32)
        for e in range(1, experts):
            other = jnp.dot(tokens[:, :width], whole[e], preferred_element_type=f32)
            total = jnp.where(chosen == e, other, total)
        total = total.astype(bf16)
        return total[:, :channels], total[:, channels:]

    @pl.when(step == 0)
    def _():
        for at, distance in zip(range(near), (0, 1, depth - 1)):
            place(slots[at], distance)
        for at in range(middle):
            distance = at + 2

            @pl.when(z >= distance)
            def _():
                place(slots[near + 2 * at], distance)

            @pl.when(z < distance)
            def _():
                place(slots[near + 2 * at + 1], distance)

        before, _ = project(edge_ref[...])
        seen[0:8, :] = before[halo - 8 :].astype(f32)
        state[...] = jnp.zeros_like(state)

    inner, gate = project(x_ref[...])
    gate_ref[...] = gate
    seen[8:, :] = inner.astype(f32)
    mixed = jnp.zeros((length, channels), f32)
    for tap in range(taps):
        mixed = mixed + taps_ref[tap : tap + 1, :] * seen[pl.ds(8 - (taps - 1) + tap, length), :]
    seen[0:8, :] = seen[pl.ds(length, 8), :]
    values = mixed / (1.0 + jnp.exp(-mixed))

    keys, queries = maps_ref[:, :width_state], maps_ref[:, width_state:]
    gram = lax.dot_general(queries, keys, (((1,), (1,)), ((), ())), preferred_element_type=f32)
    row = lax.broadcasted_iota(jnp.int32, (length, length), 0)
    col = lax.broadcasted_iota(jnp.int32, (length, length), 1)
    lower = row >= col
    gram = jnp.where(lower, gram, 0.0)
    lane = lax.broadcasted_iota(jnp.int32, (1, channels), 1)
    rounded = values.astype(bf16)
    inside, growth, ends, decay = [], 0.0, 0.0, 0.0
    reached = 0.0
    for j in range(channels // head):
        at = first_head + j
        mine = lane // head == j
        climb, size = cols_ref[:, at : at + 1], cols_ref[:, dt_lane + at : dt_lane + at + 1]
        climb_row, size_row = rows_ref[at : at + 1, :], rows_ref[dt_lane + at : dt_lane + at + 1, :]
        spread = jnp.exp(jnp.where(lower, climb - climb_row, 0.0)) * gram * size_row
        inside.append(
            jnp.dot(
                spread.astype(bf16), rounded[:, j * head : (j + 1) * head], preferred_element_type=f32
            )
        )
        last = climb[length - 1 : length]
        growth = jnp.where(mine, jnp.exp(climb), growth)
        ends = jnp.where(mine, jnp.exp(last - climb) * size, ends)
        decay = jnp.where(mine, jnp.exp(last), decay)
        reach = cols_ref[length - 1 : length, reach_lane + at : reach_lane + at + 1]
        reached = jnp.where(mine, reach, reached)
    inside = inside[0] if len(inside) == 1 else jnp.concatenate(inside, axis=1)
    carried = jnp.dot(queries, state[...].astype(bf16), preferred_element_type=f32)
    y_ref[...] = inside + growth * carried + skip_ref[...] * values
    fresh = lax.dot_general(
        keys, (ends * values).astype(bf16), (((0,), (0,)), ((), ())), preferred_element_type=f32
    )
    state[...] = decay * state[...] + fresh

    @pl.when(step == pl.num_programs(0) - 1)
    def _():
        here = slice(first_head * head, first_head * head + channels)
        for ref in earlier:
            final_ref[:, : first_head * head] = ref[...]
        final_ref[:width_state, here] = state[...].astype(bf16)
        place = lax.broadcasted_iota(jnp.int32, (16, channels), 0)
        first = reached.astype(bf16).astype(f32)
        second = (reached - first).astype(bf16).astype(f32)
        third = reached - first - second
        parts = jnp.where(place == 0, first, jnp.where(place == 1, second, third))
        final_ref[width_state:, here] = parts.astype(bf16)


def scan(z, tokens, edge, slots, middle, found, taps, skip, earlier, first_head, head, experts, depth, width, length):
    maps_all, cols, rows = found
    count, channels = tokens.shape[0], taps.shape[1]
    width_state = maps_all.shape[1] // 2
    flat = list(slots) + [part for pair in middle for part in pair]
    block = lambda *shape: pl.BlockSpec(shape, lambda b, _: (b, 0))
    final_shape = (width_state + 16, first_head * head + channels)
    return pl.pallas_call(
        functools.partial(
            scan_kernel, first_head, head, experts, depth, width, len(slots), len(middle)
        ),
        grid_spec=pltpu.PrefetchScalarGridSpec(
            num_scalar_prefetch=1,
            grid=(count // length,),
            in_specs=[block(length, tokens.shape[1]), vmem(*edge.shape)]
            + [vmem(*part.shape) for part in flat]
            + [
                block(length, maps_all.shape[1]),
                block(length, 128),
                pl.BlockSpec((rows.shape[0], length), lambda b, _: (0, b)),
                vmem(*taps.shape),
                vmem(*skip.shape),
            ]
            + [vmem(*part.shape) for part in earlier],
            out_specs=[
                block(length, channels),
                block(length, channels),
                pl.BlockSpec(final_shape, lambda b, _: (0, 0)),
            ],
            scratch_shapes=[
                pltpu.VMEM((experts, width, 2 * channels), bf16),
                pltpu.VMEM((8 + length, channels), f32),
                pltpu.VMEM((width_state, channels), f32),
            ],
        ),
        out_shape=[
            jax.ShapeDtypeStruct((count, channels), f32),
            jax.ShapeDtypeStruct((count, channels), bf16),
            jax.ShapeDtypeStruct(final_shape, bf16),
        ],
        compiler_params=params(48),
        name="scan",
    )(z, tokens, edge, *flat, maps_all, cols, rows, taps, skip, *earlier)


def norm_kernel(chunks, before, head, heads, pos_ref, maps_ref, cols_ref, gain_ref, *refs):
    ys, gates, finals = refs[:chunks], refs[chunks : 2 * chunks], refs[2 * chunks : 2 * chunks + before]
    theirs_ref, mine_ref, entering = refs[2 * chunks + before :]
    width_state = maps_ref.shape[1] // 2
    channels = mine_ref.shape[1]
    step, steps = pl.program_id(0), pl.num_programs(0)

    @pl.when(step == 0)
    def _():
        total = jnp.zeros((width_state, channels), f32)
        logs = jnp.zeros((1, channels), f32)
        for ref in finals:
            total = total + jnp.exp(logs) * ref[:width_state, :].astype(f32)
            parts = ref[width_state:, :].astype(f32)
            logs = logs + (parts[0:1] + parts[1:2] + parts[2:3])
        entering[...] = total.astype(bf16)

    lane = lax.broadcasted_iota(jnp.int32, (1, channels), 1)
    growth = 0.0
    for j in range(heads):
        reach = cols_ref[:, reach_lane + j : reach_lane + j + 1]
        growth = jnp.where(lane // head == j, jnp.exp(reach), growth)
    queries = maps_ref[:, width_state:]
    carried = growth * jnp.dot(queries, entering[...], preferred_element_type=f32)
    join = lambda parts: parts[0][...] if chunks == 1 else jnp.concatenate([p[...] for p in parts], axis=1)
    gate = join(gates).astype(f32)
    gated = (join(ys) + carried) * (gate / (1.0 + jnp.exp(-gate)))
    row = lax.broadcasted_iota(jnp.int32, (channels, channels), 0) // head
    col = lax.broadcasted_iota(jnp.int32, (channels, channels), 1) // head
    same = (row == col).astype(f32)
    square = jnp.dot(gated * gated, same, precision=highest, preferred_element_type=f32) * (1.0 / head)
    normed = (gated * lax.rsqrt(square + 1e-05) * gain_ref[...]).astype(bf16)

    @pl.when(step < steps // 2)
    def _():
        theirs_ref[...] = normed

    @pl.when(step >= steps // 2)
    def _():
        mine_ref[...] = normed


def norm(core, found, gain, ys, gates, finals, head, length):
    maps_all, cols, _ = found
    count, channels = maps_all.shape[0] // 2, gain.shape[1]
    chunks, before = len(ys), len(finals)
    steps = count // length
    at = lambda b, core: (jnp.where(b < steps, 1 - core[0], core[0]) * steps + lax.rem(b, steps), 0)
    block = lambda *shape: pl.BlockSpec(shape, at)
    return pl.pallas_call(
        functools.partial(norm_kernel, chunks, before, head, channels // head),
        grid_spec=pltpu.PrefetchScalarGridSpec(
            num_scalar_prefetch=1,
            grid=(2 * steps,),
            in_specs=[block(length, maps_all.shape[1]), block(length, 128), vmem(*gain.shape)]
            + [block(length, channels // chunks)] * (2 * chunks)
            + [vmem(*array.shape) for array in finals],
            out_specs=[
                pl.BlockSpec((length, channels), lambda b, _: (jnp.minimum(b, steps - 1), 0)),
                pl.BlockSpec((length, channels), lambda b, _: (jnp.maximum(b - steps, 0), 0)),
            ],
            scratch_shapes=[pltpu.VMEM((maps_all.shape[1] // 2, channels), bf16)],
        ),
        out_shape=[jax.ShapeDtypeStruct((count, channels), bf16)] * 2,
        compiler_params=params(32),
        name="norm",
    )(core, maps_all, cols, gain, *ys, *gates, *finals)


def out_kernel(experts, groups, planes, depth, pos_ref, ids_ref, mine_ref, other_ref, *refs):
    weights, outs = refs[:-groups], refs[-groups:]
    group, width = pos_ref[0], mine_ref.shape[0] // groups
    chunk = weights[0].shape[-1]
    pairs = []
    for s in planes:
        if s == 0 and len(weights) > 1:
            pairs.append([weights[0][...], weights[1][...]])
            continue
        z = lax.rem(pos_ref[2] - s + depth, depth)
        pairs.append([weights[0][2 * z + pos_ref[1]], weights[0][2 * z + 1 - pos_ref[1]]])
    for s in range(groups):
        rows = pl.ds(pl.multiple_of(jnp.bitwise_xor(group, s) * width, 64), width)
        chosen = ids_ref[rows, :].astype(f32)[:, 0:1]
        mine, other = mine_ref[rows, :], other_ref[rows, :]
        second = pos_ref[1] == 1
        both_halves = jnp.concatenate([jnp.where(second, other, mine), jnp.where(second, mine, other)], axis=1)
        zero = jnp.zeros_like(both_halves)
        masked = jnp.concatenate([jnp.where(chosen == e, both_halves, zero) for e in range(experts)], axis=1)
        for at, weight in enumerate(weight for pair in pairs for weight in pair):
            total = jnp.dot(masked, weight, preferred_element_type=f32)
            outs[s][:, at * chunk : (at + 1) * chunk] = total.astype(bf16)


def project_out(position, ids, mine, other, weights, planes, depth, groups):
    rows = mine.shape[0] // groups
    whole = pl.BlockSpec(memory_space=pltpu.VMEM)
    shape = jax.ShapeDtypeStruct((rows, 2 * len(planes) * weights[0].shape[-1]), bf16)
    return pl.pallas_call(
        functools.partial(out_kernel, groups // 2, groups, planes, depth),
        in_specs=[pl.BlockSpec(memory_space=pltpu.SMEM)] + [whole] * (3 + len(weights)),
        out_specs=[whole] * groups,
        out_shape=[shape] * groups,
        compiler_params=params(48),
        name="project_out",
    )(position, ids, mine, other, *weights)


def sum_kernel(depth, groups, planes, pos_ref, *refs):
    out_ref = refs[-1]
    chunk = out_ref.shape[1] // (2 * depth)
    for at, several in enumerate(planes):
        blocks = refs[at * groups : (at + 1) * groups]
        total = blocks[0][...].astype(f32)
        for block in blocks[1:]:
            total = total + block[...].astype(f32)
        total = total.astype(bf16)
        for place, s in enumerate(several):
            z = lax.rem(pos_ref[2] - s + depth, depth)
            for j in range(2):
                core = pos_ref[1] if j == 0 else 1 - pos_ref[1]
                to = pl.multiple_of((2 * z + core) * chunk, 128)
                span = slice((2 * place + j) * chunk, (2 * place + j + 1) * chunk)
                out_ref[:, pl.ds(to, chunk)] = total[:, span]


def add_up(position, blocks, planes, depth, width):
    groups, rows = len(blocks[0]), blocks[0][0].shape[0]
    flat = [block for several in blocks for block in several]
    whole = pl.BlockSpec(memory_space=pltpu.VMEM)
    return pl.pallas_call(
        functools.partial(sum_kernel, depth, groups, planes),
        in_specs=[pl.BlockSpec(memory_space=pltpu.SMEM)] + [whole] * len(flat),
        out_specs=whole,
        out_shape=jax.ShapeDtypeStruct((rows, width), bf16),
        compiler_params=params(48),
        name="add_up",
    )(position, *flat)


def spread_pieces(sent):
    return [
        shift(block, lambda z, k, e: (z, e % 2, (2 * (e // 2) + k) ^ r)) for r, block in enumerate(sent)
    ]


def arrange_kernel(blocks, by_rows, pos_ref, *refs):
    outs = refs[blocks:]
    for r, ref in enumerate(refs[:blocks]):
        to = jnp.bitwise_xor(pos_ref[0], r)
        for at, out in enumerate(outs):
            if by_rows:
                out[to] = ref[at * out.shape[1] : (at + 1) * out.shape[1], :]
                continue
            channels = out.shape[2] // 2
            for j in range(2):
                first = (j * len(outs) + at) * channels
                out[to, :, j * channels : (j + 1) * channels] = ref[:, first : first + channels]


def arrange(blocks, group, parts, by_rows):
    whole = pl.BlockSpec(memory_space=pltpu.VMEM)
    rows, width = blocks[0].shape
    shape = (len(blocks), rows // parts, width) if by_rows else (len(blocks), rows, width // parts)
    return pl.pallas_call(
        functools.partial(arrange_kernel, len(blocks), by_rows),
        in_specs=[pl.BlockSpec(memory_space=pltpu.SMEM)] + [whole] * len(blocks),
        out_specs=[whole] * parts,
        out_shape=[jax.ShapeDtypeStruct(shape, blocks[0].dtype)] * parts,
        compiler_params=params(32),
        name="arrange",
    )(group, *blocks)


def cut_kernel(pos_ref, flat_ref, *outs):
    piece = outs[0].shape[1] // 2
    half = flat_ref.shape[1] // 2
    for r, out in enumerate(outs):
        for j in range(2):
            at = pl.multiple_of(j * half + jnp.bitwise_xor(pos_ref[0], r) * piece, 128)
            out[:, j * piece : (j + 1) * piece] = flat_ref[:, pl.ds(at, piece)]


def cut(index, flat, groups):
    rows, half = flat.shape[0], flat.shape[1] // 2
    piece = half // groups
    if piece % 128:
        at = lambda j, r: j * half + jnp.bitwise_xor(index[0], r) * piece
        return [
            jnp.concatenate([lax.dynamic_slice(flat, (0, at(j, r)), (rows, piece)) for j in range(2)], axis=1)
            for r in range(groups)
        ]
    whole = pl.BlockSpec(memory_space=pltpu.VMEM)
    return pl.pallas_call(
        cut_kernel,
        in_specs=[pl.BlockSpec(memory_space=pltpu.SMEM), whole],
        out_specs=[whole] * groups,
        out_shape=[jax.ShapeDtypeStruct((rows, 2 * piece), flat.dtype)] * groups,
        compiler_params=params(32),
        name="cut",
    )(index, flat)


def on_device(
    tokens, expert_ids, damping, in_weight, out_weight, w_bc, w_dt, rate, dt_bias, d_skip, gain, conv_weight
):
    groups, parts = lax.axis_size("exp"), lax.axis_size("ctx")
    depth, experts = parts // 2, groups // 2
    group, core, z = lax.axis_index("exp"), lax.axis_index("ctx") % 2, lax.axis_index("ctx") // 2
    rows, width = tokens.shape
    half = in_weight.shape[3]
    piece = half // groups
    heads = rate.shape[0] // 2
    head = piece // heads
    count = 2 * groups * rows
    length = 256 if count % 512 == 0 else 128
    scalar = lambda v: jnp.reshape(v, (1,)).astype(jnp.int32)
    z_at, group_at, core_at = scalar(z), scalar(group), scalar(core)
    depth_weight = in_weight.shape[1]
    swap = lambda array: shift(array, lambda z, k, e: (z, 1 - k, e))
    phase = lax.optimization_barrier

    added = jnp.concatenate(
        [expert_ids.astype(bf16), damping[:, None], jnp.zeros((rows, extra - 2), bf16)], axis=1
    )
    wide = jnp.concatenate([tokens, added], axis=1)
    planes = [[2 * i * groups + j for j in range(2 * groups)] for i in range(depth)]
    flat = in_weight[0].reshape(depth_weight, 2 * half)
    index = scalar(2 * (group // 2) + core)
    got = spread_pieces(cut(index, flat, groups))
    got, wide, out_weight, w_bc, w_dt, rate, dt_bias, d_skip, gain, conv_weight = phase(
        (got, wide, out_weight, w_bc, w_dt, rate, dt_bias, d_skip, gain, conv_weight)
    )

    plane = lax.all_gather(wide, both, axis=0, tiled=True, axis_index_groups=planes)
    (shard,) = arrange(got, group_at, 1, False)
    shard = shard.reshape(groups * depth_weight, 2 * piece)
    near = line_near(shard, depth)
    columns = out_weight.shape[2]
    out_shard = lax.all_to_all(
        out_weight[0].reshape(groups, piece, columns), "exp", 0, 0, tiled=True
    ).reshape(half, columns)
    local = lambda vector: lax.dynamic_slice_in_dim(vector, core * heads, heads, 0)
    lanes = lambda vector: jnp.concatenate(
        [jnp.pad(local(vector), (0, dt_lane - heads))] * (128 // dt_lane)
    )[None, :]
    picked = lax.dynamic_slice_in_dim(w_dt, (2 * group + core) * heads, heads, 0)
    picked = jnp.concatenate([jnp.pad(picked, ((0, dt_lane - heads), (0, 0)))] * (128 // dt_lane), axis=0)
    w_maps = jnp.concatenate([w_bc, picked.T], axis=1)
    bias_lanes, rate_lanes = lanes(dt_bias), lanes(rate)
    half_taps = lax.dynamic_slice_in_dim(conv_weight, core * piece, piece, 1)
    half_gain = lax.dynamic_slice_in_dim(gain, core * piece, piece, 0)[None, :]
    half_skip = jnp.repeat(local(d_skip), head)[None, :]
    shard, near, out_shard, w_maps, bias_lanes, rate_lanes, half_taps, half_gain, half_skip = phase(
        (shard, near, out_shard, w_maps, bias_lanes, rate_lanes, half_taps, half_gain, half_skip)
    )

    far = line_far(near, depth)
    edge = shift(plane[count - halo :], lambda z, k, e: (z + 1, k, e) if z + 1 < depth else None)
    found = maps(plane, w_maps, bias_lanes, rate_lanes, heads, w_bc.shape[1], length)
    ids = lax.dynamic_slice(plane, (core * groups * rows, width), (groups * rows, extra))
    far, plane, edge, found, out_shard, ids = phase((far, plane, edge, found, out_shard, ids))

    whole_out = lax.all_gather(out_shard, "ctx", axis=0)
    y, gate, final = scan(
        z_at, plane, edge, [shard, *near], far, found, half_taps, half_skip,
        [], 0, head, experts, depth, width, length,
    )
    y, gate, final, out_shard = phase((y, gate, final, out_shard))

    finals = [
        shift(final, lambda z, k, e: (z + s, k, e) if z + s < depth else None) for s in range(1, depth)
    ]
    theirs, mine = norm(core_at, found, half_gain, [y], [gate], finals, head, length)
    out_other = swap(out_shard)
    theirs, out_other = phase((theirs, out_other))
    other = swap(theirs)
    other, mine = phase((other, mine))

    position = jnp.concatenate([group_at, core_at, z_at])

    def send(weights, planes):
        results = project_out(position, ids, mine, other, weights, planes, depth, groups)
        return [results[0]] + [
            shift(results[r], lambda z, k, e: (z, k, e ^ r)) for r in range(1, groups)
        ]

    order = [(0,), tuple(range(1, depth))]
    blocks = [send([out_shard, out_other], order[0])]
    whole_out, blocks = phase((whole_out, blocks))
    blocks.append(send([whole_out], order[1]))
    return add_up(position, blocks, order, depth, width)


def solution(mesh):
    placed = (
        P(("ctx", "exp"), None),
        P(("ctx", "exp"), None),
        P(("ctx", "exp")),
        P("exp", "ctx", None, None),
        P("exp", None, "ctx"),
        P(),
        P(),
        P("exp"),
        P("exp"),
        P("exp"),
        P("exp"),
        P(None, "exp"),
    )
    return jax.shard_map(
        on_device, mesh=mesh, in_specs=placed, out_specs=P(("ctx", "exp"), None), check_vma=False
    )
```

```python
import functools

import jax
import jax.numpy as jnp
from jax import lax
from jax.experimental import pallas as pl
from jax.experimental.pallas import tpu as pltpu
from jax.sharding import PartitionSpec as P

both = ("ctx", "exp")
extra = 128
halo = 16
dt_lane, reach_lane = 16, 32
highest = lax.Precision.HIGHEST
f32, bf16 = jnp.float32, jnp.bfloat16


def params(mib):
    return pltpu.CompilerParams(vmem_limit_bytes=mib << 20)


def vmem(*shape):
    return pl.BlockSpec(shape, lambda *_: (0,) * len(shape), pipeline_mode=pl.Buffered(1))


def shift(array, move):
    groups = lax.axis_size("exp")
    pairs = []
    for c in range(lax.axis_size("ctx")):
        for e in range(groups):
            to = move(c // 2, c % 2, e)
            if to is not None:
                pairs.append((c * groups + e, (2 * to[0] + to[1]) * groups + to[2]))
    return lax.ppermute(array, both, pairs)


def line_near(own, depth):
    return (
        shift(own, lambda z, k, e: ((z + 1) % depth, k, e)),
        shift(own, lambda z, k, e: ((z - 1) % depth, k, e)),
    )


def step_up(array, s, depth):
    return shift(array, lambda z, k, e: (z + 1, k, e) if s - 1 <= z < depth - 1 else None)


def step_down(array, s, depth):
    return shift(array, lambda z, k, e: (z - 1, k, e) if 0 < z <= depth - s else None)


def line_far(near, depth):
    ups, downs = [], []
    up, down = near
    for s in range(2, depth - 1):
        up, down = step_up(up, s, depth), step_down(down, s, depth)
        ups.append(up)
        downs.append(down)
    return paired(ups, downs)


def paired(ups, downs):
    return list(zip(ups, downs[::-1]))


def maps_kernel(heads, width, x_ref, w_ref, bias_ref, rate_ref, maps_ref, cols_ref, rows_ref, total):
    length = x_ref.shape[0]

    @pl.when(pl.program_id(0) == 0)
    def _():
        total[...] = jnp.zeros_like(total)

    found = jnp.dot(x_ref[:, :width], w_ref[...], preferred_element_type=f32).astype(bf16)
    state2 = maps_ref.shape[1]
    maps_ref[...] = found[:, :state2]
    raw = found[:, state2:].astype(f32) + bias_ref[...]
    steps = jnp.maximum(raw, 0.0) + jnp.log1p(jnp.exp(-jnp.abs(raw)))
    damping = x_ref[:, width : width + extra].astype(f32)[:, 1:2]
    logs = -(rate_ref[...] * steps + damping)
    row = lax.broadcasted_iota(jnp.int32, (length, length), 0)
    col = lax.broadcasted_iota(jnp.int32, (length, length), 1)
    lower = (row >= col).astype(f32)
    climb = jnp.dot(lower, logs, precision=highest, preferred_element_type=f32)
    lane = lax.broadcasted_iota(jnp.int32, climb.shape, 1)
    reach = climb + total[...]
    packed = jnp.where(lane < dt_lane, climb, jnp.where(lane < reach_lane, steps, reach))
    cols_ref[...] = packed
    rows_ref[...] = jnp.transpose(packed)[: rows_ref.shape[0]]
    total[...] = reach[length - 1 : length]


def maps(tokens, w_maps, bias, rate, heads, state2, length):
    count, width = tokens.shape[0], w_maps.shape[0]
    return pl.pallas_call(
        functools.partial(maps_kernel, heads, width),
        grid=(count // length,),
        in_specs=[
            pl.BlockSpec((length, tokens.shape[1]), lambda b: (b, 0)),
            vmem(*w_maps.shape),
            vmem(1, 128),
            vmem(1, 128),
        ],
        out_specs=[
            pl.BlockSpec((length, state2), lambda b: (b, 0)),
            pl.BlockSpec((length, 128), lambda b: (b, 0)),
            pl.BlockSpec((reach_lane, length), lambda b: (0, b)),
        ],
        out_shape=[
            jax.ShapeDtypeStruct((count, state2), bf16),
            jax.ShapeDtypeStruct((count, 128), f32),
            jax.ShapeDtypeStruct((reach_lane, count), f32),
        ],
        scratch_shapes=[pltpu.VMEM((1, 128), f32)],
        compiler_params=params(32),
        name="maps",
    )(tokens, w_maps, bias, rate)


def scan_kernel(
    first_head, head, experts, depth, width, near, middle, pos_ref, x_ref, edge_ref, *refs
):
    slots = refs[: near + 2 * middle]
    maps_ref, cols_ref, rows_ref, taps_ref, skip_ref = refs[near + 2 * middle :][:5]
    earlier = refs[near + 2 * middle + 5 : -6]
    y_ref, gate_ref, final_ref, whole, seen, state = refs[-6:]
    length, channels = y_ref.shape
    taps = taps_ref.shape[0]
    width_state = maps_ref.shape[1] // 2
    step, z = pl.program_id(0), pos_ref[0]
    depth_rows = width // depth

    def place(ref, distance):
        rows = pl.ds(pl.multiple_of(lax.rem(z - distance + depth, depth) * depth_rows, 128), depth_rows)
        for e in range(experts):
            whole[e, rows, :] = ref[e * depth_rows : (e + 1) * depth_rows, :]

    def project(tokens):
        chosen = tokens[:, width : width + extra].astype(f32)[:, 0:1]
        total = jnp.dot(tokens[:, :width], whole[0], preferred_element_type=f32)
        for e in range(1, experts):
            other = jnp.dot(tokens[:, :width], whole[e], preferred_element_type=f32)
            total = jnp.where(chosen == e, other, total)
        total = total.astype(bf16)
        return total[:, :channels], total[:, channels:]

    @pl.when(step == 0)
    def _():
        for at, distance in zip(range(near), (0, 1, depth - 1)):
            place(slots[at], distance)
        for at in range(middle):
            distance = at + 2

            @pl.when(z >= distance)
            def _():
                place(slots[near + 2 * at], distance)

            @pl.when(z < distance)
            def _():
                place(slots[near + 2 * at + 1], distance)

        before, _ = project(edge_ref[...])
        seen[0:8, :] = before[halo - 8 :].astype(f32)
        state[...] = jnp.zeros_like(state)

    inner, gate = project(x_ref[...])
    gate_ref[...] = gate
    seen[8:, :] = inner.astype(f32)
    mixed = jnp.zeros((length, channels), f32)
    for tap in range(taps):
        mixed = mixed + taps_ref[tap : tap + 1, :] * seen[pl.ds(8 - (taps - 1) + tap, length), :]
    seen[0:8, :] = seen[pl.ds(length, 8), :]
    values = mixed / (1.0 + jnp.exp(-mixed))

    keys, queries = maps_ref[:, :width_state], maps_ref[:, width_state:]
    gram = lax.dot_general(queries, keys, (((1,), (1,)), ((), ())), preferred_element_type=f32)
    row = lax.broadcasted_iota(jnp.int32, (length, length), 0)
    col = lax.broadcasted_iota(jnp.int32, (length, length), 1)
    lower = row >= col
    gram = jnp.where(lower, gram, 0.0)
    lane = lax.broadcasted_iota(jnp.int32, (1, channels), 1)
    rounded = values.astype(bf16)
    inside, growth, ends, decay = [], 0.0, 0.0, 0.0
    reached = 0.0
    for j in range(channels // head):
        at = first_head + j
        mine = lane // head == j
        climb, size = cols_ref[:, at : at + 1], cols_ref[:, dt_lane + at : dt_lane + at + 1]
        climb_row, size_row = rows_ref[at : at + 1, :], rows_ref[dt_lane + at : dt_lane + at + 1, :]
        spread = jnp.exp(jnp.where(lower, climb - climb_row, 0.0)) * gram * size_row
        inside.append(
            jnp.dot(
                spread.astype(bf16), rounded[:, j * head : (j + 1) * head], preferred_element_type=f32
            )
        )
        last = climb[length - 1 : length]
        growth = jnp.where(mine, jnp.exp(climb), growth)
        ends = jnp.where(mine, jnp.exp(last - climb) * size, ends)
        decay = jnp.where(mine, jnp.exp(last), decay)
        reach = cols_ref[length - 1 : length, reach_lane + at : reach_lane + at + 1]
        reached = jnp.where(mine, reach, reached)
    inside = inside[0] if len(inside) == 1 else jnp.concatenate(inside, axis=1)
    carried = jnp.dot(queries, state[...].astype(bf16), preferred_element_type=f32)
    y_ref[...] = inside + growth * carried + skip_ref[...] * values
    fresh = lax.dot_general(
        keys, (ends * values).astype(bf16), (((0,), (0,)), ((), ())), preferred_element_type=f32
    )
    state[...] = decay * state[...] + fresh

    @pl.when(step == pl.num_programs(0) - 1)
    def _():
        here = slice(first_head * head, first_head * head + channels)
        for ref in earlier:
            final_ref[:, : first_head * head] = ref[...]
        final_ref[:width_state, here] = state[...].astype(bf16)
        place = lax.broadcasted_iota(jnp.int32, (16, channels), 0)
        first = reached.astype(bf16).astype(f32)
        second = (reached - first).astype(bf16).astype(f32)
        third = reached - first - second
        parts = jnp.where(place == 0, first, jnp.where(place == 1, second, third))
        final_ref[width_state:, here] = parts.astype(bf16)


def scan(z, tokens, edge, slots, middle, found, taps, skip, earlier, first_head, head, experts, depth, width, length):
    maps_all, cols, rows = found
    count, channels = tokens.shape[0], taps.shape[1]
    width_state = maps_all.shape[1] // 2
    flat = list(slots) + [part for pair in middle for part in pair]
    block = lambda *shape: pl.BlockSpec(shape, lambda b, _: (b, 0))
    final_shape = (width_state + 16, first_head * head + channels)
    return pl.pallas_call(
        functools.partial(
            scan_kernel, first_head, head, experts, depth, width, len(slots), len(middle)
        ),
        grid_spec=pltpu.PrefetchScalarGridSpec(
            num_scalar_prefetch=1,
            grid=(count // length,),
            in_specs=[block(length, tokens.shape[1]), vmem(*edge.shape)]
            + [vmem(*part.shape) for part in flat]
            + [
                block(length, maps_all.shape[1]),
                block(length, 128),
                pl.BlockSpec((rows.shape[0], length), lambda b, _: (0, b)),
                vmem(*taps.shape),
                vmem(*skip.shape),
            ]
            + [vmem(*part.shape) for part in earlier],
            out_specs=[
                block(length, channels),
                block(length, channels),
                pl.BlockSpec(final_shape, lambda b, _: (0, 0)),
            ],
            scratch_shapes=[
                pltpu.VMEM((experts, width, 2 * channels), bf16),
                pltpu.VMEM((8 + length, channels), f32),
                pltpu.VMEM((width_state, channels), f32),
            ],
        ),
        out_shape=[
            jax.ShapeDtypeStruct((count, channels), f32),
            jax.ShapeDtypeStruct((count, channels), bf16),
            jax.ShapeDtypeStruct(final_shape, bf16),
        ],
        compiler_params=params(48),
        name="scan",
    )(z, tokens, edge, *flat, maps_all, cols, rows, taps, skip, *earlier)


def norm_kernel(chunks, before, head, heads, pos_ref, maps_ref, cols_ref, gain_ref, *refs):
    ys, gates, finals = refs[:chunks], refs[chunks : 2 * chunks], refs[2 * chunks : 2 * chunks + before]
    theirs_ref, mine_ref, entering = refs[2 * chunks + before :]
    width_state = maps_ref.shape[1] // 2
    channels = mine_ref.shape[1]
    step, steps = pl.program_id(0), pl.num_programs(0)

    @pl.when(step == 0)
    def _():
        total = jnp.zeros((width_state, channels), f32)
        logs = jnp.zeros((1, channels), f32)
        for ref in finals:
            total = total + jnp.exp(logs) * ref[:width_state, :].astype(f32)
            parts = ref[width_state:, :].astype(f32)
            logs = logs + (parts[0:1] + parts[1:2] + parts[2:3])
        entering[...] = total.astype(bf16)

    lane = lax.broadcasted_iota(jnp.int32, (1, channels), 1)
    growth = 0.0
    for j in range(heads):
        reach = cols_ref[:, reach_lane + j : reach_lane + j + 1]
        growth = jnp.where(lane // head == j, jnp.exp(reach), growth)
    queries = maps_ref[:, width_state:]
    carried = growth * jnp.dot(queries, entering[...], preferred_element_type=f32)
    join = lambda parts: parts[0][...] if chunks == 1 else jnp.concatenate([p[...] for p in parts], axis=1)
    gate = join(gates).astype(f32)
    gated = (join(ys) + carried) * (gate / (1.0 + jnp.exp(-gate)))
    row = lax.broadcasted_iota(jnp.int32, (channels, channels), 0) // head
    col = lax.broadcasted_iota(jnp.int32, (channels, channels), 1) // head
    same = (row == col).astype(f32)
    square = jnp.dot(gated * gated, same, precision=highest, preferred_element_type=f32) * (1.0 / head)
    normed = (gated * lax.rsqrt(square + 1e-05) * gain_ref[...]).astype(bf16)

    @pl.when(step < steps // 2)
    def _():
        theirs_ref[...] = normed

    @pl.when(step >= steps // 2)
    def _():
        mine_ref[...] = normed


def norm(core, found, gain, ys, gates, finals, head, length):
    maps_all, cols, _ = found
    count, channels = maps_all.shape[0] // 2, gain.shape[1]
    chunks, before = len(ys), len(finals)
    steps = count // length
    at = lambda b, core: (jnp.where(b < steps, 1 - core[0], core[0]) * steps + lax.rem(b, steps), 0)
    block = lambda *shape: pl.BlockSpec(shape, at)
    return pl.pallas_call(
        functools.partial(norm_kernel, chunks, before, head, channels // head),
        grid_spec=pltpu.PrefetchScalarGridSpec(
            num_scalar_prefetch=1,
            grid=(2 * steps,),
            in_specs=[block(length, maps_all.shape[1]), block(length, 128), vmem(*gain.shape)]
            + [block(length, channels // chunks)] * (2 * chunks)
            + [vmem(*array.shape) for array in finals],
            out_specs=[
                pl.BlockSpec((length, channels), lambda b, _: (jnp.minimum(b, steps - 1), 0)),
                pl.BlockSpec((length, channels), lambda b, _: (jnp.maximum(b - steps, 0), 0)),
            ],
            scratch_shapes=[pltpu.VMEM((maps_all.shape[1] // 2, channels), bf16)],
        ),
        out_shape=[jax.ShapeDtypeStruct((count, channels), bf16)] * 2,
        compiler_params=params(32),
        name="norm",
    )(core, maps_all, cols, gain, *ys, *gates, *finals)


def out_kernel(experts, groups, pos_ref, ids_ref, mine_ref, other_ref, *refs):
    weights, outs = refs[:-groups], refs[-groups:]
    group, width = pos_ref[0], mine_ref.shape[0] // groups
    chunk = weights[0].shape[1]
    for s in range(groups):
        rows = pl.ds(pl.multiple_of(jnp.bitwise_xor(group, s) * width, 64), width)
        chosen = ids_ref[rows, :].astype(f32)[:, 0:1]
        mine, other = mine_ref[rows, :], other_ref[rows, :]
        second = pos_ref[1] == 1
        both_halves = jnp.concatenate([jnp.where(second, other, mine), jnp.where(second, mine, other)], axis=1)
        zero = jnp.zeros_like(both_halves)
        masked = jnp.concatenate([jnp.where(chosen == e, both_halves, zero) for e in range(experts)], axis=1)
        for at, weight in enumerate(weights):
            total = jnp.dot(masked, weight[...], preferred_element_type=f32)
            outs[s][:, at * chunk : (at + 1) * chunk] = total.astype(bf16)


def project_out(position, ids, mine, other, weights, groups):
    rows = mine.shape[0] // groups
    whole = pl.BlockSpec(memory_space=pltpu.VMEM)
    shape = jax.ShapeDtypeStruct((rows, len(weights) * weights[0].shape[1]), bf16)
    return pl.pallas_call(
        functools.partial(out_kernel, groups // 2, groups),
        in_specs=[pl.BlockSpec(memory_space=pltpu.SMEM)] + [whole] * (3 + len(weights)),
        out_specs=[whole] * groups,
        out_shape=[shape] * groups,
        compiler_params=params(48),
        name="project_out",
    )(position, ids, mine, other, *weights)


def sum_kernel(depth, groups, distances, pos_ref, *refs):
    out_ref = refs[-1]
    chunk = out_ref.shape[1] // (2 * depth)
    for at, several in enumerate(distances):
        blocks = refs[at * groups : (at + 1) * groups]
        total = blocks[0][...].astype(f32)
        for block in blocks[1:]:
            total = total + block[...].astype(f32)
        total = total.astype(bf16)
        for place, distance in enumerate(several):
            z = lax.rem(pos_ref[0] - distance + depth, depth)
            for j in range(2):
                core = pos_ref[1] if j == 0 else 1 - pos_ref[1]
                to = pl.multiple_of((2 * z + core) * chunk, 128)
                span = slice((2 * place + j) * chunk, (2 * place + j + 1) * chunk)
                out_ref[:, pl.ds(to, chunk)] = total[:, span]


def add_up(position, blocks, distances, depth, width):
    groups, rows = len(blocks[0]), blocks[0][0].shape[0]
    flat = [block for several in blocks for block in several]
    whole = pl.BlockSpec(memory_space=pltpu.VMEM)
    return pl.pallas_call(
        functools.partial(sum_kernel, depth, groups, distances),
        in_specs=[pl.BlockSpec(memory_space=pltpu.SMEM)] + [whole] * len(flat),
        out_specs=whole,
        out_shape=jax.ShapeDtypeStruct((rows, width), bf16),
        compiler_params=params(48),
        name="add_up",
    )(position, *flat)


def spread_pieces(sent):
    return [
        shift(block, lambda z, k, e: (z, e % 2, (2 * (e // 2) + k) ^ r)) for r, block in enumerate(sent)
    ]


def arrange_kernel(blocks, by_rows, pos_ref, *refs):
    outs = refs[blocks:]
    for r, ref in enumerate(refs[:blocks]):
        to = jnp.bitwise_xor(pos_ref[0], r)
        for at, out in enumerate(outs):
            if by_rows:
                out[to] = ref[at * out.shape[1] : (at + 1) * out.shape[1], :]
                continue
            channels = out.shape[2] // 2
            for j in range(2):
                first = (j * len(outs) + at) * channels
                out[to, :, j * channels : (j + 1) * channels] = ref[:, first : first + channels]


def arrange(blocks, group, parts, by_rows):
    whole = pl.BlockSpec(memory_space=pltpu.VMEM)
    rows, width = blocks[0].shape
    shape = (len(blocks), rows // parts, width) if by_rows else (len(blocks), rows, width // parts)
    return pl.pallas_call(
        functools.partial(arrange_kernel, len(blocks), by_rows),
        in_specs=[pl.BlockSpec(memory_space=pltpu.SMEM)] + [whole] * len(blocks),
        out_specs=[whole] * parts,
        out_shape=[jax.ShapeDtypeStruct(shape, blocks[0].dtype)] * parts,
        compiler_params=params(32),
        name="arrange",
    )(group, *blocks)


def cut_rows_kernel(sources, pos_ref, *refs):
    for r, out in enumerate(refs[sources:]):
        piece = out.shape[0] // sources
        rows = pl.ds(pl.multiple_of(jnp.bitwise_xor(pos_ref[0], r) * piece, 64), piece)
        for at, ref in enumerate(refs[:sources]):
            out[at * piece : (at + 1) * piece, :] = ref[rows, :]


def cut_rows(group, arrays, groups):
    whole = pl.BlockSpec(memory_space=pltpu.VMEM)
    rows, width = arrays[0].shape
    shape = (len(arrays) * rows // groups, width)
    return pl.pallas_call(
        functools.partial(cut_rows_kernel, len(arrays)),
        in_specs=[pl.BlockSpec(memory_space=pltpu.SMEM)] + [whole] * len(arrays),
        out_specs=[whole] * groups,
        out_shape=[jax.ShapeDtypeStruct(shape, arrays[0].dtype)] * groups,
        compiler_params=params(32),
        name="cut_rows",
    )(group, *arrays)


def cut_kernel(pos_ref, flat_ref, *outs):
    piece = outs[0].shape[1] // 2
    half = flat_ref.shape[1] // 2
    for r, out in enumerate(outs):
        for j in range(2):
            at = pl.multiple_of(j * half + jnp.bitwise_xor(pos_ref[0], r) * piece, 128)
            out[:, j * piece : (j + 1) * piece] = flat_ref[:, pl.ds(at, piece)]


def cut(index, flat, groups):
    rows, half = flat.shape[0], flat.shape[1] // 2
    piece = half // groups
    if piece % 128:
        at = lambda j, r: j * half + jnp.bitwise_xor(index[0], r) * piece
        return [
            jnp.concatenate([lax.dynamic_slice(flat, (0, at(j, r)), (rows, piece)) for j in range(2)], axis=1)
            for r in range(groups)
        ]
    whole = pl.BlockSpec(memory_space=pltpu.VMEM)
    return pl.pallas_call(
        cut_kernel,
        in_specs=[pl.BlockSpec(memory_space=pltpu.SMEM), whole],
        out_specs=[whole] * groups,
        out_shape=[jax.ShapeDtypeStruct((rows, 2 * piece), flat.dtype)] * groups,
        compiler_params=params(32),
        name="cut",
    )(index, flat)


def lay_kernel(pos_ref, *refs):
    blocks, whole, sems = refs[:-2], refs[-2], refs[-1]
    rows = blocks[0].shape[0]
    copies = []
    for at, block in enumerate(blocks):
        row = pl.multiple_of(jnp.bitwise_xor(pos_ref[0], at) * rows, 64)
        copies.append(pltpu.make_async_copy(block, whole.at[pl.ds(row, rows), :], sems.at[at]))
    for copy in copies:
        copy.start()
    for copy in copies:
        copy.wait()


def lay(position, blocks):
    rows, width = blocks[0].shape
    place = pl.BlockSpec(memory_space=pl.ANY)
    return pl.pallas_call(
        lay_kernel,
        in_specs=[pl.BlockSpec(memory_space=pltpu.SMEM)] + [place] * len(blocks),
        out_specs=place,
        out_shape=jax.ShapeDtypeStruct((len(blocks) * rows, width), blocks[0].dtype),
        scratch_shapes=[pltpu.SemaphoreType.DMA((len(blocks),))],
        compiler_params=params(16),
        name="lay",
    )(position, *blocks)


def on_device(
    tokens, expert_ids, damping, in_weight, out_weight, w_bc, w_dt, rate, dt_bias, d_skip, gain, conv_weight
):
    groups, parts = lax.axis_size("exp"), lax.axis_size("ctx")
    depth, experts = parts // 2, groups // 2
    group, core, z = lax.axis_index("exp"), lax.axis_index("ctx") % 2, lax.axis_index("ctx") // 2
    rows, width = tokens.shape
    half = in_weight.shape[3]
    piece = half // groups
    heads = rate.shape[0] // 2
    head = piece // heads
    count = 2 * groups * rows
    length = 256 if count % 512 == 0 else 128
    scalar = lambda v: jnp.reshape(v, (1,)).astype(jnp.int32)
    z_at, group_at, core_at = scalar(z), scalar(group), scalar(core)
    depth_weight = in_weight.shape[1]
    swap = lambda array: shift(array, lambda z, k, e: (z, 1 - k, e))
    phase = lax.optimization_barrier

    flat = in_weight[0].reshape(depth_weight, 2 * half)
    index = scalar(2 * (group // 2) + core)
    got = spread_pieces(cut(index, flat, groups))
    out_raw = [out_weight[0], shift(out_weight[0], lambda z, k, e: ((z - 1) % depth, k, e))]
    added = jnp.concatenate(
        [expert_ids.astype(bf16), damping[:, None], jnp.zeros((rows, extra - 2), bf16)], axis=1
    )
    wide = jnp.concatenate([tokens, added], axis=1)
    got, wide, out_raw, w_bc, w_dt, rate, dt_bias, d_skip, gain, conv_weight = phase(
        (got, wide, out_raw, w_bc, w_dt, rate, dt_bias, d_skip, gain, conv_weight)
    )

    (shard,) = arrange(got, group_at, 1, False)
    shard = shard.reshape(groups * depth_weight, 2 * piece)
    near = line_near(shard, depth)
    wide, out_raw = phase((wide, out_raw, shard))[:2]
    exchange = lambda array, r: shift(array, lambda z, k, e: (z, k, e ^ r))
    own = [wide] + [exchange(wide, r) for r in range(1, groups)]
    local = lambda vector: lax.dynamic_slice_in_dim(vector, core * heads, heads, 0)
    lanes = lambda vector: jnp.concatenate(
        [jnp.pad(local(vector), (0, dt_lane - heads))] * (128 // dt_lane)
    )[None, :]
    picked = lax.dynamic_slice_in_dim(w_dt, (2 * group + core) * heads, heads, 0)
    picked = jnp.concatenate([jnp.pad(picked, ((0, dt_lane - heads), (0, 0)))] * (128 // dt_lane), axis=0)
    w_maps = jnp.concatenate([w_bc, picked.T], axis=1)
    bias_lanes, rate_lanes = lanes(dt_bias), lanes(rate)
    half_taps = lax.dynamic_slice_in_dim(conv_weight, core * piece, piece, 1)
    half_gain = lax.dynamic_slice_in_dim(gain, core * piece, piece, 0)[None, :]
    half_skip = jnp.repeat(local(d_skip), head)[None, :]
    out_sent = cut_rows(group_at, out_raw, groups)
    out_got = [out_sent[0]]
    for r in range(1, groups):
        own[r], block = phase((own[r], out_sent[r]))
        out_got.append(exchange(block, r))
    columns = out_weight.shape[2]
    part = lay(group_at, own)
    out_shard, above = [array.reshape(half, columns) for array in arrange(out_got, group_at, 2, True)]
    shard, near, part, out_shard, above, w_maps, bias_lanes, rate_lanes, half_taps, half_gain, half_skip = phase(
        (shard, near, part, out_shard, above, w_maps, bias_lanes, rate_lanes, half_taps, half_gain, half_skip)
    )

    far = line_far(near, depth)
    other_part = swap(part)
    plane = lay(core_at, [part, other_part])
    edge = shift(plane[count - halo :], lambda z, k, e: (z + 1, k, e) if z + 1 < depth else None)
    found = maps(plane, w_maps, bias_lanes, rate_lanes, heads, w_bc.shape[1], length)
    ids = lax.dynamic_slice(plane, (core * groups * rows, width), (groups * rows, extra))
    out_shard, above, _ = phase((out_shard, above, other_part))
    out_shard_other, above_other = swap(out_shard), swap(above)
    far, plane, edge, found, ids, out_shard, above, out_shard_other, above_other = phase(
        (far, plane, edge, found, ids, out_shard, above, out_shard_other, above_other)
    )

    y, gate, final = scan(
        z_at, plane, edge, [shard, *near], far, found, half_taps, half_skip,
        [], 0, head, experts, depth, width, length,
    )
    below = shift(out_shard, lambda z, k, e: ((z + 1) % depth, k, e))
    y, gate, final, below = phase((y, gate, final, below))

    finals = [
        shift(final, lambda z, k, e: (z + s, k, e) if z + s < depth else None) for s in range(1, depth)
    ]
    ups, downs = [below], [above]
    for s in range(2, depth - 1):
        ups.append(step_up(ups[-1], s, depth))
        downs.append(step_down(downs[-1], s, depth))
    theirs, mine = norm(core_at, found, half_gain, [y], [gate], finals, head, length)
    theirs, mine, below = phase((theirs, mine, below))
    other = swap(theirs)
    below_other = swap(below)
    other, mine = phase((other, mine))

    position = jnp.concatenate([group_at, core_at])

    def send(*weights):
        results = project_out(position, ids, mine, other, weights, groups)
        return [results[0]] + [exchange(results[r], r) for r in range(1, groups)]

    blocks = [send(out_shard, out_shard_other, above, above_other)]
    ups, downs, below_other, blocks[0][0] = phase((ups, downs, below_other, blocks[0][0]))
    late = [jnp.where(z >= s + 2, up, down) for s, (up, down) in enumerate(paired(ups[1:], downs[1:]))]
    blocks.append(send(below, below_other, *[array for part in late for array in (part, swap(part))]))
    distances = [(0, depth - 1), (1, *range(2, depth - 1))]
    return add_up(jnp.concatenate([z_at, core_at]), blocks, distances, depth, width)


def solution(mesh):
    placed = (
        P(("ctx", "exp"), None),
        P(("ctx", "exp"), None),
        P(("ctx", "exp")),
        P("exp", "ctx", None, None),
        P("exp", None, "ctx"),
        P(),
        P(),
        P("exp"),
        P("exp"),
        P("exp"),
        P("exp"),
        P(None, "exp"),
    )
    return jax.shard_map(
        on_device, mesh=mesh, in_specs=placed, out_specs=P(("ctx", "exp"), None), check_vma=False
    )
```

```python
import functools

import jax
import jax.numpy as jnp
from jax import lax
from jax.experimental import pallas as pl
from jax.experimental.pallas import tpu as pltpu
from jax.sharding import PartitionSpec as P

both = ("ctx", "exp")
extra = 128
halo = 16
dt_lane, reach_lane = 16, 32
highest = lax.Precision.HIGHEST
f32, bf16 = jnp.float32, jnp.bfloat16


def params(mib):
    return pltpu.CompilerParams(vmem_limit_bytes=mib << 20)


def vmem(*shape):
    return pl.BlockSpec(shape, lambda *_: (0,) * len(shape), pipeline_mode=pl.Buffered(1))


def shift(array, move):
    groups = lax.axis_size("exp")
    pairs = []
    for c in range(lax.axis_size("ctx")):
        for e in range(groups):
            to = move(c // 2, c % 2, e)
            if to is not None:
                pairs.append((c * groups + e, (2 * to[0] + to[1]) * groups + to[2]))
    return lax.ppermute(array, both, pairs)


def line_near(own, depth):
    return (
        shift(own, lambda z, k, e: ((z + 1) % depth, k, e)),
        shift(own, lambda z, k, e: ((z - 1) % depth, k, e)),
    )


def step_up(array, s, depth):
    return shift(array, lambda z, k, e: (z + 1, k, e) if s - 1 <= z < depth - 1 else None)


def step_down(array, s, depth):
    return shift(array, lambda z, k, e: (z - 1, k, e) if 0 < z <= depth - s else None)


def line_far(near, depth):
    ups, downs = [], []
    up, down = near
    for s in range(2, depth - 1):
        up, down = step_up(up, s, depth), step_down(down, s, depth)
        ups.append(up)
        downs.append(down)
    return paired(ups, downs)


def paired(ups, downs):
    return list(zip(ups, downs[::-1]))


def slice_of(z, distance, depth, rows):
    return pl.multiple_of(lax.rem(z - distance + depth, depth) * rows, 128)


def choose(extra_lanes, parts):
    chosen = extra_lanes.astype(f32)[:, 0:1]
    total = parts[0]
    for e in range(1, len(parts)):
        total = jnp.where(chosen == e, parts[e], total)
    return total


def ahead_kernel(experts, depth, width, distances, pos_ref, x_ref, w_ref, bias_ref, rate_ref, *refs):
    slots, (part_ref, maps_ref, cols_ref, rows_ref, total) = refs[: len(distances)], refs[len(distances) :]
    length = x_ref.shape[0]

    @pl.when(pl.program_id(0) == 0)
    def _():
        total[...] = jnp.zeros_like(total)

    added = x_ref[:, width:]
    found = jnp.dot(x_ref[:, :width], w_ref[...], preferred_element_type=f32).astype(bf16)
    state2 = maps_ref.shape[1]
    maps_ref[...] = found[:, :state2]
    raw = found[:, state2:].astype(f32) + bias_ref[...]
    steps = jnp.maximum(raw, 0.0) + jnp.log1p(jnp.exp(-jnp.abs(raw)))
    logs = -(rate_ref[...] * steps + added.astype(f32)[:, 1:2])
    first = logs.astype(bf16)
    second = (logs - first.astype(f32)).astype(bf16)
    third = (logs - first.astype(f32) - second.astype(f32)).astype(bf16)
    row = lax.broadcasted_iota(jnp.int32, (length, length), 0)
    col = lax.broadcasted_iota(jnp.int32, (length, length), 1)
    lower = (row >= col).astype(bf16)
    sums = jnp.dot(lower, jnp.concatenate([first, second, third], axis=1), preferred_element_type=f32)
    climb = sums[:, :128] + (sums[:, 128:256] + sums[:, 256:])
    lane = lax.broadcasted_iota(jnp.int32, climb.shape, 1)
    reach = climb + total[...]
    packed = jnp.where(lane < dt_lane, climb, jnp.where(lane < reach_lane, steps, reach))
    cols_ref[...] = packed
    rows_ref[...] = jnp.transpose(packed)[: rows_ref.shape[0]]
    total[...] = reach[length - 1 : length]

    depth_rows = width // depth
    parts = []
    for e in range(experts):
        part = 0.0
        for distance, slot in zip(distances, slots):
            x = x_ref[:, pl.ds(slice_of(pos_ref[0], distance, depth, depth_rows), depth_rows)]
            part += jnp.dot(x, slot[e * depth_rows : (e + 1) * depth_rows, :], preferred_element_type=f32)
        parts.append(part)
    part_ref[...] = choose(added, parts)


def ahead(position, tokens, w_maps, bias, rate, slots, distances, experts, depth, state2, length):
    count, width, columns = tokens.shape[0], w_maps.shape[0], slots[0].shape[1]
    block = lambda *shape: pl.BlockSpec(shape, lambda b, _: (b, 0))
    return pl.pallas_call(
        functools.partial(ahead_kernel, experts, depth, width, distances),
        grid_spec=pltpu.PrefetchScalarGridSpec(
            num_scalar_prefetch=1,
            grid=(count // length,),
            in_specs=[block(length, tokens.shape[1])]
            + [vmem(*w_maps.shape), vmem(1, 128), vmem(1, 128)]
            + [vmem(*slot.shape) for slot in slots],
            out_specs=[
                block(length, columns),
                block(length, state2),
                block(length, 128),
                pl.BlockSpec((reach_lane, length), lambda b, _: (0, b)),
            ],
            scratch_shapes=[pltpu.VMEM((1, 128), f32)],
        ),
        out_shape=[
            jax.ShapeDtypeStruct((count, columns), f32),
            jax.ShapeDtypeStruct((count, state2), bf16),
            jax.ShapeDtypeStruct((count, 128), f32),
            jax.ShapeDtypeStruct((reach_lane, count), f32),
        ],
        compiler_params=params(40),
        name="ahead",
    )(position, tokens, w_maps, bias, rate, *slots)


def scan_kernel(head, experts, depth, width, distances, middle, pos_ref, *refs):
    near, count = len(distances), len(middle)
    slots, pairs = refs[:near], refs[near : near + 2 * count]
    xs, refs = refs[near + 2 * count : near + 3 * count], refs[near + 3 * count :]
    extra_ref, edge_ref, part_ref, maps_ref, cols_ref, rows_ref, taps_ref, skip_ref = refs[:8]
    y_ref, gate_ref, final_ref, nears, fars, seen, state, sems = refs[8:]
    length, channels = y_ref.shape
    taps = taps_ref.shape[0]
    width_state = maps_ref.shape[1] // 2
    step, z = pl.program_id(0), pos_ref[0]
    depth_rows = width // depth
    near_copies = [pltpu.make_async_copy(slots[i], nears.at[i], sems.at[i]) for i in range(near)]

    def far(m, action):
        up, down = (
            pltpu.make_async_copy(pairs[2 * m + i], fars.at[m], sems.at[near + m]) for i in range(2)
        )

        @pl.when(z >= middle[m])
        def _():
            action(up)

        @pl.when(z < middle[m])
        def _():
            action(down)

    def expert(ref, e):
        return ref[e * depth_rows : (e + 1) * depth_rows, :]

    @pl.when(step == 0)
    def _():
        for m in range(count):
            far(m, lambda copy: copy.start())
        for copy in near_copies:
            copy.start()
        state[...] = jnp.zeros_like(state)
        for m in range(count):
            far(m, lambda copy: copy.wait())
        for copy in near_copies:
            copy.wait()
        parts = []
        for e in range(experts):
            total = 0.0
            for distance, ref in [(d, nears.at[i]) for i, d in enumerate(distances)] + [
                (d, fars.at[i]) for i, d in enumerate(middle)
            ]:
                x = edge_ref[:, pl.ds(slice_of(z, distance, depth, depth_rows), depth_rows)]
                total += jnp.dot(x, expert(ref, e), preferred_element_type=f32)
            parts.append(total)
        before = choose(edge_ref[:, width:], parts).astype(bf16)
        seen[0:8, :] = before[halo - 8 :, :channels].astype(f32)

    parts = []
    for e in range(experts):
        total = 0.0
        for m in range(count):
            total += jnp.dot(xs[m][...], expert(fars.at[m], e), preferred_element_type=f32)
        parts.append(total)
    whole = (part_ref[...] + choose(extra_ref[...], parts)).astype(bf16)
    gate_ref[...] = whole[:, channels:]
    seen[8:, :] = whole[:, :channels].astype(f32)
    mixed = jnp.zeros((length, channels), f32)
    for tap in range(taps):
        mixed = mixed + taps_ref[tap : tap + 1, :] * seen[pl.ds(8 - (taps - 1) + tap, length), :]
    seen[0:8, :] = seen[pl.ds(length, 8), :]
    values = mixed / (1.0 + jnp.exp(-mixed))

    keys, queries = maps_ref[:, :width_state], maps_ref[:, width_state:]
    gram = lax.dot_general(queries, keys, (((1,), (1,)), ((), ())), preferred_element_type=f32)
    row = lax.broadcasted_iota(jnp.int32, (length, length), 0)
    col = lax.broadcasted_iota(jnp.int32, (length, length), 1)
    lower = row >= col
    gram = jnp.where(lower, gram, 0.0)
    lane = lax.broadcasted_iota(jnp.int32, (1, channels), 1)
    rounded = values.astype(bf16)
    inside, growth, ends, decay, reached = [], 0.0, 0.0, 0.0, 0.0
    for j in range(channels // head):
        mine = lane // head == j
        climb, size = cols_ref[:, j : j + 1], cols_ref[:, dt_lane + j : dt_lane + j + 1]
        climb_row, size_row = rows_ref[j : j + 1, :], rows_ref[dt_lane + j : dt_lane + j + 1, :]
        spread = jnp.exp(jnp.where(lower, climb - climb_row, 0.0)) * gram * size_row
        inside.append(
            jnp.dot(
                spread.astype(bf16), rounded[:, j * head : (j + 1) * head], preferred_element_type=f32
            )
        )
        last = climb[length - 1 : length]
        growth = jnp.where(mine, jnp.exp(climb), growth)
        ends = jnp.where(mine, jnp.exp(last - climb) * size, ends)
        decay = jnp.where(mine, jnp.exp(last), decay)
        reach = cols_ref[length - 1 : length, reach_lane + j : reach_lane + j + 1]
        reached = jnp.where(mine, reach, reached)
    inside = inside[0] if len(inside) == 1 else jnp.concatenate(inside, axis=1)
    carried = jnp.dot(queries, state[...].astype(bf16), preferred_element_type=f32)
    y_ref[...] = inside + growth * carried + skip_ref[...] * values
    fresh = lax.dot_general(
        keys, (ends * values).astype(bf16), (((0,), (0,)), ((), ())), preferred_element_type=f32
    )
    state[...] = decay * state[...] + fresh

    @pl.when(step == pl.num_programs(0) - 1)
    def _():
        final_ref[:width_state, :] = state[...].astype(bf16)
        place = lax.broadcasted_iota(jnp.int32, (16, channels), 0)
        first = reached.astype(bf16).astype(f32)
        second = (reached - first).astype(bf16).astype(f32)
        third = reached - first - second
        parts = jnp.where(place == 0, first, jnp.where(place == 1, second, third))
        final_ref[width_state:, :] = parts.astype(bf16)


def scan(z, tokens, edge, slots, distances, middle, part, found, taps, skip, head, experts, depth, width, length):
    maps_all, cols, rows = found
    count, channels = tokens.shape[0], taps.shape[1]
    width_state = maps_all.shape[1] // 2
    far_distances = tuple(range(2, 2 + len(middle)))
    flat = [array for pair in middle for array in pair]
    block = lambda *shape: pl.BlockSpec(shape, lambda b, _: (b, 0))
    depth_rows = width // depth

    def columns_of(distance):
        return pl.BlockSpec(
            (length, depth_rows), lambda b, at: (b, lax.rem(at[0] - distance + depth, depth))
        )

    final_shape = (width_state + 16, channels)
    return pl.pallas_call(
        functools.partial(scan_kernel, head, experts, depth, width, distances, far_distances),
        grid_spec=pltpu.PrefetchScalarGridSpec(
            num_scalar_prefetch=1,
            grid=(count // length,),
            in_specs=[pl.BlockSpec(memory_space=pl.ANY)] * (len(slots) + len(flat))
            + [columns_of(distance) for distance in far_distances]
            + [
                pl.BlockSpec((length, extra), lambda b, _: (b, width // extra)),
                vmem(*edge.shape),
                block(length, part.shape[1]),
                block(length, maps_all.shape[1]),
                block(length, 128),
                pl.BlockSpec((rows.shape[0], length), lambda b, _: (0, b)),
                vmem(*taps.shape),
                vmem(*skip.shape),
            ],
            out_specs=[
                block(length, channels),
                block(length, channels),
                pl.BlockSpec(final_shape, lambda b, _: (0, 0)),
            ],
            scratch_shapes=[
                pltpu.VMEM((len(slots),) + slots[0].shape, bf16),
                pltpu.VMEM((len(middle),) + slots[0].shape, bf16),
                pltpu.VMEM((8 + length, channels), f32),
                pltpu.VMEM((width_state, channels), f32),
                pltpu.SemaphoreType.DMA((len(slots) + len(middle),)),
            ],
        ),
        out_shape=[
            jax.ShapeDtypeStruct((count, channels), f32),
            jax.ShapeDtypeStruct((count, channels), bf16),
            jax.ShapeDtypeStruct(final_shape, bf16),
        ],
        compiler_params=params(40),
        name="scan",
    )(z, *slots, *flat, *[tokens] * len(far_distances), tokens, edge, part, maps_all, cols, rows, taps, skip)


def norm_kernel(chunks, before, head, heads, pos_ref, maps_ref, cols_ref, gain_ref, *refs):
    ys, gates, finals = refs[:chunks], refs[chunks : 2 * chunks], refs[2 * chunks : 2 * chunks + before]
    theirs_ref, mine_ref, entering = refs[2 * chunks + before :]
    width_state = maps_ref.shape[1] // 2
    channels = mine_ref.shape[1]
    step, steps = pl.program_id(0), pl.num_programs(0)

    @pl.when(step == 0)
    def _():
        total = jnp.zeros((width_state, channels), f32)
        logs = jnp.zeros((1, channels), f32)
        for ref in finals:
            total = total + jnp.exp(logs) * ref[:width_state, :].astype(f32)
            parts = ref[width_state:, :].astype(f32)
            logs = logs + (parts[0:1] + parts[1:2] + parts[2:3])
        entering[...] = total.astype(bf16)

    lane = lax.broadcasted_iota(jnp.int32, (1, channels), 1)
    growth = 0.0
    for j in range(heads):
        reach = cols_ref[:, reach_lane + j : reach_lane + j + 1]
        growth = jnp.where(lane // head == j, jnp.exp(reach), growth)
    queries = maps_ref[:, width_state:]
    carried = growth * jnp.dot(queries, entering[...], preferred_element_type=f32)
    join = lambda parts: parts[0][...] if chunks == 1 else jnp.concatenate([p[...] for p in parts], axis=1)
    gate = join(gates).astype(f32)
    gated = (join(ys) + carried) * (gate / (1.0 + jnp.exp(-gate)))
    row = lax.broadcasted_iota(jnp.int32, (channels, channels), 0) // head
    col = lax.broadcasted_iota(jnp.int32, (channels, channels), 1) // head
    same = (row == col).astype(bf16)
    squares = gated * gated
    first = squares.astype(bf16)
    second = (squares - first.astype(f32)).astype(bf16)
    square = jnp.dot(first, same, preferred_element_type=f32) + jnp.dot(second, same, preferred_element_type=f32)
    square = square * (1.0 / head)
    normed = (gated * lax.rsqrt(square + 1e-05) * gain_ref[...]).astype(bf16)

    @pl.when(step < steps // 2)
    def _():
        theirs_ref[...] = normed

    @pl.when(step >= steps // 2)
    def _():
        mine_ref[...] = normed


def norm(core, found, gain, ys, gates, finals, head, length):
    maps_all, cols, _ = found
    count, channels = maps_all.shape[0] // 2, gain.shape[1]
    chunks, before = len(ys), len(finals)
    steps = count // length
    at = lambda b, core: (jnp.where(b < steps, 1 - core[0], core[0]) * steps + lax.rem(b, steps), 0)
    block = lambda *shape: pl.BlockSpec(shape, at)
    return pl.pallas_call(
        functools.partial(norm_kernel, chunks, before, head, channels // head),
        grid_spec=pltpu.PrefetchScalarGridSpec(
            num_scalar_prefetch=1,
            grid=(2 * steps,),
            in_specs=[block(length, maps_all.shape[1]), block(length, 128), vmem(*gain.shape)]
            + [block(length, channels // chunks)] * (2 * chunks)
            + [vmem(*array.shape) for array in finals],
            out_specs=[
                pl.BlockSpec((length, channels), lambda b, _: (jnp.minimum(b, steps - 1), 0)),
                pl.BlockSpec((length, channels), lambda b, _: (jnp.maximum(b - steps, 0), 0)),
            ],
            scratch_shapes=[pltpu.VMEM((maps_all.shape[1] // 2, channels), bf16)],
        ),
        out_shape=[jax.ShapeDtypeStruct((count, channels), bf16)] * 2,
        compiler_params=params(32),
        name="norm",
    )(core, maps_all, cols, gain, *ys, *gates, *finals)


def out_kernel(experts, groups, pos_ref, ids_ref, mine_ref, other_ref, *refs):
    weights, outs = refs[:-groups], refs[-groups:]
    group, width = pos_ref[0], mine_ref.shape[0] // groups
    chunk = weights[0].shape[1]
    for s in range(groups):
        rows = pl.ds(pl.multiple_of(jnp.bitwise_xor(group, s) * width, 64), width)
        chosen = ids_ref[rows, :].astype(f32)[:, 0:1]
        mine, other = mine_ref[rows, :], other_ref[rows, :]
        second = pos_ref[1] == 1
        both_halves = jnp.concatenate([jnp.where(second, other, mine), jnp.where(second, mine, other)], axis=1)
        zero = jnp.zeros_like(both_halves)
        masked = jnp.concatenate([jnp.where(chosen == e, both_halves, zero) for e in range(experts)], axis=1)
        for at, weight in enumerate(weights):
            total = jnp.dot(masked, weight[...], preferred_element_type=f32)
            outs[s][:, at * chunk : (at + 1) * chunk] = total.astype(bf16)


def project_out(position, ids, mine, other, weights, groups):
    rows = mine.shape[0] // groups
    whole = pl.BlockSpec(memory_space=pltpu.VMEM)
    shape = jax.ShapeDtypeStruct((rows, len(weights) * weights[0].shape[1]), bf16)
    return pl.pallas_call(
        functools.partial(out_kernel, groups // 2, groups),
        in_specs=[pl.BlockSpec(memory_space=pltpu.SMEM)] + [whole] * (3 + len(weights)),
        out_specs=[whole] * groups,
        out_shape=[shape] * groups,
        compiler_params=params(48),
        name="project_out",
    )(position, ids, mine, other, *weights)


def sum_kernel(depth, groups, distances, pos_ref, *refs):
    out_ref = refs[-1]
    chunk = out_ref.shape[1] // (2 * depth)
    for at, several in enumerate(distances):
        blocks = refs[at * groups : (at + 1) * groups]
        total = blocks[0][...].astype(f32)
        for block in blocks[1:]:
            total = total + block[...].astype(f32)
        total = total.astype(bf16)
        for place, distance in enumerate(several):
            z = lax.rem(pos_ref[0] - distance + depth, depth)
            for j in range(2):
                core = pos_ref[1] if j == 0 else 1 - pos_ref[1]
                to = pl.multiple_of((2 * z + core) * chunk, 128)
                span = slice((2 * place + j) * chunk, (2 * place + j + 1) * chunk)
                out_ref[:, pl.ds(to, chunk)] = total[:, span]


def add_up(position, blocks, distances, depth, width):
    groups, rows = len(blocks[0]), blocks[0][0].shape[0]
    flat = [block for several in blocks for block in several]
    whole = pl.BlockSpec(memory_space=pltpu.VMEM)
    return pl.pallas_call(
        functools.partial(sum_kernel, depth, groups, distances),
        in_specs=[pl.BlockSpec(memory_space=pltpu.SMEM)] + [whole] * len(flat),
        out_specs=whole,
        out_shape=jax.ShapeDtypeStruct((rows, width), bf16),
        compiler_params=params(48),
        name="add_up",
    )(position, *flat)


def spread_pieces(sent):
    return [
        shift(block, lambda z, k, e: (z, e % 2, (2 * (e // 2) + k) ^ r)) for r, block in enumerate(sent)
    ]


def arrange_kernel(blocks, by_rows, pos_ref, *refs):
    outs = refs[blocks:]
    for r, ref in enumerate(refs[:blocks]):
        to = jnp.bitwise_xor(pos_ref[0], r)
        for at, out in enumerate(outs):
            if by_rows:
                out[to] = ref[at * out.shape[1] : (at + 1) * out.shape[1], :]
                continue
            channels = out.shape[2] // 2
            for j in range(2):
                first = (j * len(outs) + at) * channels
                out[to, :, j * channels : (j + 1) * channels] = ref[:, first : first + channels]


def arrange(blocks, group, parts, by_rows):
    whole = pl.BlockSpec(memory_space=pltpu.VMEM)
    rows, width = blocks[0].shape
    shape = (len(blocks), rows // parts, width) if by_rows else (len(blocks), rows, width // parts)
    return pl.pallas_call(
        functools.partial(arrange_kernel, len(blocks), by_rows),
        in_specs=[pl.BlockSpec(memory_space=pltpu.SMEM)] + [whole] * len(blocks),
        out_specs=[whole] * parts,
        out_shape=[jax.ShapeDtypeStruct(shape, blocks[0].dtype)] * parts,
        compiler_params=params(32),
        name="arrange",
    )(group, *blocks)


def cut_rows_kernel(sources, pos_ref, *refs):
    for r, out in enumerate(refs[sources:]):
        piece = out.shape[0] // sources
        rows = pl.ds(pl.multiple_of(jnp.bitwise_xor(pos_ref[0], r) * piece, 64), piece)
        for at, ref in enumerate(refs[:sources]):
            out[at * piece : (at + 1) * piece, :] = ref[rows, :]


def cut_rows(group, arrays, groups):
    whole = pl.BlockSpec(memory_space=pltpu.VMEM)
    rows, width = arrays[0].shape
    shape = (len(arrays) * rows // groups, width)
    return pl.pallas_call(
        functools.partial(cut_rows_kernel, len(arrays)),
        in_specs=[pl.BlockSpec(memory_space=pltpu.SMEM)] + [whole] * len(arrays),
        out_specs=[whole] * groups,
        out_shape=[jax.ShapeDtypeStruct(shape, arrays[0].dtype)] * groups,
        compiler_params=params(32),
        name="cut_rows",
    )(group, *arrays)


def cut_kernel(pos_ref, flat_ref, *outs):
    piece = outs[0].shape[1] // 2
    half = flat_ref.shape[1] // 2
    for r, out in enumerate(outs):
        for j in range(2):
            at = pl.multiple_of(j * half + jnp.bitwise_xor(pos_ref[0], r) * piece, 128)
            out[:, j * piece : (j + 1) * piece] = flat_ref[:, pl.ds(at, piece)]


def cut(index, flat, groups):
    rows, half = flat.shape[0], flat.shape[1] // 2
    piece = half // groups
    if piece % 128:
        at = lambda j, r: j * half + jnp.bitwise_xor(index[0], r) * piece
        return [
            jnp.concatenate([lax.dynamic_slice(flat, (0, at(j, r)), (rows, piece)) for j in range(2)], axis=1)
            for r in range(groups)
        ]
    whole = pl.BlockSpec(memory_space=pltpu.VMEM)
    return pl.pallas_call(
        cut_kernel,
        in_specs=[pl.BlockSpec(memory_space=pltpu.SMEM), whole],
        out_specs=[whole] * groups,
        out_shape=[jax.ShapeDtypeStruct((rows, 2 * piece), flat.dtype)] * groups,
        compiler_params=params(32),
        name="cut",
    )(index, flat)


def lay_kernel(pos_ref, *refs):
    blocks, whole, sems = refs[:-2], refs[-2], refs[-1]
    rows = blocks[0].shape[0]
    copies = []
    for at, block in enumerate(blocks):
        row = pl.multiple_of(jnp.bitwise_xor(pos_ref[0], at) * rows, 64)
        copies.append(pltpu.make_async_copy(block, whole.at[pl.ds(row, rows), :], sems.at[at]))
    for copy in copies:
        copy.start()
    for copy in copies:
        copy.wait()


def lay(position, blocks):
    rows, width = blocks[0].shape
    place = pl.BlockSpec(memory_space=pl.ANY)
    return pl.pallas_call(
        lay_kernel,
        in_specs=[pl.BlockSpec(memory_space=pltpu.SMEM)] + [place] * len(blocks),
        out_specs=place,
        out_shape=jax.ShapeDtypeStruct((len(blocks) * rows, width), blocks[0].dtype),
        scratch_shapes=[pltpu.SemaphoreType.DMA((len(blocks),))],
        compiler_params=params(16),
        name="lay",
    )(position, *blocks)


def on_device(
    tokens, expert_ids, damping, in_weight, out_weight, w_bc, w_dt, rate, dt_bias, d_skip, gain, conv_weight
):
    groups, parts = lax.axis_size("exp"), lax.axis_size("ctx")
    depth, experts = parts // 2, groups // 2
    group, core, z = lax.axis_index("exp"), lax.axis_index("ctx") % 2, lax.axis_index("ctx") // 2
    rows, width = tokens.shape
    half = in_weight.shape[3]
    piece = half // groups
    heads = rate.shape[0] // 2
    head = piece // heads
    count = 2 * groups * rows
    length = 256 if count % 512 == 0 else 128
    scalar = lambda v: jnp.reshape(v, (1,)).astype(jnp.int32)
    z_at, group_at, core_at = scalar(z), scalar(group), scalar(core)
    depth_weight = in_weight.shape[1]
    swap = lambda array: shift(array, lambda z, k, e: (z, 1 - k, e))
    phase = lax.optimization_barrier

    flat = in_weight[0].reshape(depth_weight, 2 * half)
    index = scalar(2 * (group // 2) + core)
    got = spread_pieces(cut(index, flat, groups))
    out_raw = [out_weight[0], shift(out_weight[0], lambda z, k, e: ((z - 1) % depth, k, e))]
    added = jnp.concatenate(
        [expert_ids.astype(bf16), damping[:, None], jnp.zeros((rows, extra - 2), bf16)], axis=1
    )
    wide = jnp.concatenate([tokens, added], axis=1)
    got, wide, out_raw, w_bc, w_dt, rate, dt_bias, d_skip, gain, conv_weight = phase(
        (got, wide, out_raw, w_bc, w_dt, rate, dt_bias, d_skip, gain, conv_weight)
    )

    (shard,) = arrange(got, group_at, 1, False)
    shard = shard.reshape(groups * depth_weight, 2 * piece)
    near = line_near(shard, depth)
    wide, out_raw = phase((wide, out_raw, shard))[:2]
    exchange = lambda array, r: shift(array, lambda z, k, e: (z, k, e ^ r))
    own = [wide] + [exchange(wide, r) for r in range(1, groups)]
    local = lambda vector: lax.dynamic_slice_in_dim(vector, core * heads, heads, 0)
    lanes = lambda vector: jnp.concatenate(
        [jnp.pad(local(vector), (0, dt_lane - heads))] * (128 // dt_lane)
    )[None, :]
    picked = lax.dynamic_slice_in_dim(w_dt, (2 * group + core) * heads, heads, 0)
    picked = jnp.concatenate([jnp.pad(picked, ((0, dt_lane - heads), (0, 0)))] * (128 // dt_lane), axis=0)
    w_maps = jnp.concatenate([w_bc, picked.T], axis=1)
    bias_lanes, rate_lanes = lanes(dt_bias), lanes(rate)
    half_taps = lax.dynamic_slice_in_dim(conv_weight, core * piece, piece, 1)
    half_gain = lax.dynamic_slice_in_dim(gain, core * piece, piece, 0)[None, :]
    half_skip = jnp.repeat(local(d_skip), head)[None, :]
    out_sent = cut_rows(group_at, out_raw, groups)
    out_got = [out_sent[0]]
    for r in range(1, groups):
        own[r], block = phase((own[r], out_sent[r]))
        out_got.append(exchange(block, r))
    columns = out_weight.shape[2]
    part = lay(group_at, own)
    out_shard, above = [array.reshape(half, columns) for array in arrange(out_got, group_at, 2, True)]
    shard, near, part, out_shard, above, w_maps, bias_lanes, rate_lanes, half_taps, half_gain, half_skip = phase(
        (shard, near, part, out_shard, above, w_maps, bias_lanes, rate_lanes, half_taps, half_gain, half_skip)
    )

    far = line_far(near, depth)
    other_part = swap(part)
    plane = lay(core_at, [part, other_part])
    edge = shift(plane[count - halo :], lambda z, k, e: (z + 1, k, e) if z + 1 < depth else None)
    ids = lax.dynamic_slice(plane, (core * groups * rows, width), (groups * rows, extra))
    slots, distances = [shard, *near], (0, 1, depth - 1)
    part, *found = ahead(
        z_at, plane, w_maps, bias_lanes, rate_lanes, slots, distances, experts, depth, w_bc.shape[1], length
    )
    out_shard, above, _ = phase((out_shard, above, other_part))
    out_shard_other, above_other = swap(out_shard), swap(above)
    far, plane, edge, found, part, ids, out_shard, above, out_shard_other, above_other = phase(
        (far, plane, edge, found, part, ids, out_shard, above, out_shard_other, above_other)
    )

    y, gate, final = scan(
        z_at, plane, edge, slots, distances, far, part, found, half_taps, half_skip,
        head, experts, depth, width, length,
    )
    below = shift(out_shard, lambda z, k, e: ((z + 1) % depth, k, e))
    y, gate, final, below = phase((y, gate, final, below))

    finals = [
        shift(final, lambda z, k, e: (z + s, k, e) if z + s < depth else None) for s in range(1, depth)
    ]
    ups, downs = [below], [above]
    for s in range(2, depth - 1):
        ups.append(step_up(ups[-1], s, depth))
        downs.append(step_down(downs[-1], s, depth))
    theirs, mine = norm(core_at, found, half_gain, [y], [gate], finals, head, length)
    theirs, mine, below = phase((theirs, mine, below))
    other = swap(theirs)
    below_other = swap(below)
    other, mine = phase((other, mine))

    position = jnp.concatenate([group_at, core_at])

    def send(*weights):
        results = project_out(position, ids, mine, other, weights, groups)
        return [results[0]] + [exchange(results[r], r) for r in range(1, groups)]

    blocks = [send(out_shard, out_shard_other, above, above_other)]
    ups, downs, below_other, blocks[0][0] = phase((ups, downs, below_other, blocks[0][0]))
    late = [jnp.where(z >= s + 2, up, down) for s, (up, down) in enumerate(paired(ups[1:], downs[1:]))]
    blocks.append(send(below, below_other, *[array for part in late for array in (part, swap(part))]))
    order = [(0, depth - 1), (1, *range(2, depth - 1))]
    return add_up(jnp.concatenate([z_at, core_at]), blocks, order, depth, width)


def solution(mesh):
    placed = (
        P(("ctx", "exp"), None),
        P(("ctx", "exp"), None),
        P(("ctx", "exp")),
        P("exp", "ctx", None, None),
        P("exp", None, "ctx"),
        P(),
        P(),
        P("exp"),
        P("exp"),
        P("exp"),
        P("exp"),
        P(None, "exp"),
    )
    return jax.shard_map(
        on_device, mesh=mesh, in_specs=placed, out_specs=P(("ctx", "exp"), None), check_vma=False
    )
```

```python
import functools

import jax
import jax.numpy as jnp
from jax import lax
from jax.experimental import pallas as pl
from jax.experimental.pallas import tpu as pltpu
from jax.sharding import PartitionSpec as P

both = ("ctx", "exp")
extra = 128
halo = 16
dt_lane, reach_lane = 16, 32
highest = lax.Precision.HIGHEST
f32, bf16 = jnp.float32, jnp.bfloat16


def params(mib):
    return pltpu.CompilerParams(vmem_limit_bytes=mib << 20)


def vmem(*shape):
    return pl.BlockSpec(shape, lambda *_: (0,) * len(shape), pipeline_mode=pl.Buffered(1))


def shift(array, move):
    groups = lax.axis_size("exp")
    pairs = []
    for c in range(lax.axis_size("ctx")):
        for e in range(groups):
            to = move(c // 2, c % 2, e)
            if to is not None:
                pairs.append((c * groups + e, (2 * to[0] + to[1]) * groups + to[2]))
    return lax.ppermute(array, both, pairs)


def line_near(own, depth):
    return (
        shift(own, lambda z, k, e: ((z + 1) % depth, k, e)),
        shift(own, lambda z, k, e: ((z - 1) % depth, k, e)),
    )


def step_up(array, s, depth):
    return shift(array, lambda z, k, e: (z + 1, k, e) if s - 1 <= z < depth - 1 else None)


def step_down(array, s, depth):
    return shift(array, lambda z, k, e: (z - 1, k, e) if 0 < z <= depth - s else None)


def line_far(near, depth):
    ups, downs = [], []
    up, down = near
    for s in range(2, depth - 1):
        up, down = step_up(up, s, depth), step_down(down, s, depth)
        ups.append(up)
        downs.append(down)
    return paired(ups, downs)


def paired(ups, downs):
    return list(zip(ups, downs[::-1]))


def slice_of(z, distance, depth, rows):
    return pl.multiple_of(lax.rem(z - distance + depth, depth) * rows, 128)


def choose(extra_lanes, parts):
    chosen = extra_lanes.astype(f32)[:, 0:1]
    total = parts[0]
    for e in range(1, len(parts)):
        total = jnp.where(chosen == e, parts[e], total)
    return total


def ahead_kernel(experts, depth, width, distances, pos_ref, x_ref, w_ref, bias_ref, rate_ref, *refs):
    slots, (part_ref, maps_ref, cols_ref, rows_ref, total) = refs[: len(distances)], refs[len(distances) :]
    length = x_ref.shape[0]

    @pl.when(pl.program_id(0) == 0)
    def _():
        total[...] = jnp.zeros_like(total)

    added = x_ref[:, width:]
    found = jnp.dot(x_ref[:, :width], w_ref[...], preferred_element_type=f32).astype(bf16)
    state2 = maps_ref.shape[1]
    maps_ref[...] = found[:, :state2]
    raw = found[:, state2:].astype(f32) + bias_ref[...]
    steps = jnp.maximum(raw, 0.0) + jnp.log1p(jnp.exp(-jnp.abs(raw)))
    logs = -(rate_ref[...] * steps + added.astype(f32)[:, 1:2])
    first = logs.astype(bf16)
    second = (logs - first.astype(f32)).astype(bf16)
    third = (logs - first.astype(f32) - second.astype(f32)).astype(bf16)
    row = lax.broadcasted_iota(jnp.int32, (length, length), 0)
    col = lax.broadcasted_iota(jnp.int32, (length, length), 1)
    lower = (row >= col).astype(bf16)
    sums = jnp.dot(lower, jnp.concatenate([first, second, third], axis=1), preferred_element_type=f32)
    climb = sums[:, :128] + (sums[:, 128:256] + sums[:, 256:])
    lane = lax.broadcasted_iota(jnp.int32, climb.shape, 1)
    reach = climb + total[...]
    packed = jnp.where(lane < dt_lane, climb, jnp.where(lane < reach_lane, steps, reach))
    cols_ref[...] = packed
    rows_ref[...] = jnp.transpose(packed)[: rows_ref.shape[0]]
    total[...] = reach[length - 1 : length]

    depth_rows = width // depth
    parts = []
    for e in range(experts):
        part = 0.0
        for distance, slot in zip(distances, slots):
            x = x_ref[:, pl.ds(slice_of(pos_ref[0], distance, depth, depth_rows), depth_rows)]
            part += jnp.dot(x, slot[e * depth_rows : (e + 1) * depth_rows, :], preferred_element_type=f32)
        parts.append(part)
    part_ref[...] = choose(added, parts)


def ahead(position, tokens, w_maps, bias, rate, slots, distances, experts, depth, state2, length):
    count, width, columns = tokens.shape[0], w_maps.shape[0], slots[0].shape[1]
    block = lambda *shape: pl.BlockSpec(shape, lambda b, _: (b, 0))
    return pl.pallas_call(
        functools.partial(ahead_kernel, experts, depth, width, distances),
        grid_spec=pltpu.PrefetchScalarGridSpec(
            num_scalar_prefetch=1,
            grid=(count // length,),
            in_specs=[block(length, tokens.shape[1])]
            + [vmem(*w_maps.shape), vmem(1, 128), vmem(1, 128)]
            + [vmem(*slot.shape) for slot in slots],
            out_specs=[
                block(length, columns),
                block(length, state2),
                block(length, 128),
                pl.BlockSpec((reach_lane, length), lambda b, _: (0, b)),
            ],
            scratch_shapes=[pltpu.VMEM((1, 128), f32)],
        ),
        out_shape=[
            jax.ShapeDtypeStruct((count, columns), f32),
            jax.ShapeDtypeStruct((count, state2), bf16),
            jax.ShapeDtypeStruct((count, 128), f32),
            jax.ShapeDtypeStruct((reach_lane, count), f32),
        ],
        compiler_params=params(40),
        name="ahead",
    )(position, tokens, w_maps, bias, rate, *slots)


def scan_kernel(head, experts, depth, width, distances, middle, pos_ref, *refs):
    near, count = len(distances), len(middle)
    slots, pairs = refs[:near], refs[near : near + 2 * count]
    xs, refs = refs[near + 2 * count : near + 3 * count], refs[near + 3 * count :]
    extra_ref, edge_ref, part_ref, maps_ref, cols_ref, rows_ref, taps_ref, skip_ref = refs[:8]
    y_ref, gate_ref, final_ref, nears, fars, seen, state, sems = refs[8:]
    length, channels = y_ref.shape
    taps = taps_ref.shape[0]
    width_state = maps_ref.shape[1] // 2
    step, z = pl.program_id(0), pos_ref[0]
    depth_rows = width // depth
    near_copies = [pltpu.make_async_copy(slots[i], nears.at[i], sems.at[i]) for i in range(near)]

    def far(m, action):
        up, down = (
            pltpu.make_async_copy(pairs[2 * m + i], fars.at[m], sems.at[near + m]) for i in range(2)
        )

        @pl.when(z >= middle[m])
        def _():
            action(up)

        @pl.when(z < middle[m])
        def _():
            action(down)

    def expert(ref, e):
        return ref[e * depth_rows : (e + 1) * depth_rows, :]

    @pl.when(step == 0)
    def _():
        for m in range(count):
            far(m, lambda copy: copy.start())
        for copy in near_copies:
            copy.start()
        state[...] = jnp.zeros_like(state)
        for m in range(count):
            far(m, lambda copy: copy.wait())
        for copy in near_copies:
            copy.wait()
        parts = []
        for e in range(experts):
            total = 0.0
            for distance, ref in [(d, nears.at[i]) for i, d in enumerate(distances)] + [
                (d, fars.at[i]) for i, d in enumerate(middle)
            ]:
                x = edge_ref[:, pl.ds(slice_of(z, distance, depth, depth_rows), depth_rows)]
                total += jnp.dot(x, expert(ref, e), preferred_element_type=f32)
            parts.append(total)
        before = choose(edge_ref[:, width:], parts).astype(bf16).astype(f32)
        seen[0:8, :] = before[halo - 8 :, :channels]

    parts = []
    for e in range(experts):
        total = 0.0
        for m in range(count):
            total += jnp.dot(xs[m][...], expert(fars.at[m], e), preferred_element_type=f32)
        parts.append(total)
    whole = (part_ref[...] + choose(extra_ref[...], parts)).astype(bf16)
    gate_ref[...] = whole[:, channels:]
    seen[8:, :] = whole[:, :channels].astype(f32)
    mixed = jnp.zeros((length, channels), f32)
    for tap in range(taps):
        mixed = mixed + taps_ref[tap : tap + 1, :] * seen[pl.ds(8 - (taps - 1) + tap, length), :]
    seen[0:8, :] = seen[pl.ds(length, 8), :]
    values = mixed / (1.0 + jnp.exp(-mixed))

    keys, queries = maps_ref[:, :width_state], maps_ref[:, width_state:]
    gram = lax.dot_general(queries, keys, (((1,), (1,)), ((), ())), preferred_element_type=f32)
    row = lax.broadcasted_iota(jnp.int32, (length, length), 0)
    col = lax.broadcasted_iota(jnp.int32, (length, length), 1)
    lower = row >= col
    gram = jnp.where(lower, gram, 0.0)
    lane = lax.broadcasted_iota(jnp.int32, (1, channels), 1)
    rounded = values.astype(bf16)
    inside, growth, ends, decay, reached = [], 0.0, 0.0, 0.0, 0.0
    for j in range(channels // head):
        mine = lane // head == j
        climb, size = cols_ref[:, j : j + 1], cols_ref[:, dt_lane + j : dt_lane + j + 1]
        climb_row, size_row = rows_ref[j : j + 1, :], rows_ref[dt_lane + j : dt_lane + j + 1, :]
        spread = jnp.exp(jnp.where(lower, climb - climb_row, 0.0)) * gram * size_row
        inside.append(
            jnp.dot(
                spread.astype(bf16), rounded[:, j * head : (j + 1) * head], preferred_element_type=f32
            )
        )
        last = climb[length - 1 : length]
        growth = jnp.where(mine, jnp.exp(climb), growth)
        ends = jnp.where(mine, jnp.exp(last - climb) * size, ends)
        decay = jnp.where(mine, jnp.exp(last), decay)
        reach = cols_ref[length - 1 : length, reach_lane + j : reach_lane + j + 1]
        reached = jnp.where(mine, reach, reached)
    inside = inside[0] if len(inside) == 1 else jnp.concatenate(inside, axis=1)
    carried = jnp.dot(queries, state[...].astype(bf16), preferred_element_type=f32)
    y_ref[...] = inside + growth * carried + skip_ref[...] * values
    fresh = lax.dot_general(
        keys, (ends * values).astype(bf16), (((0,), (0,)), ((), ())), preferred_element_type=f32
    )
    state[...] = decay * state[...] + fresh

    @pl.when(step == pl.num_programs(0) - 1)
    def _():
        final_ref[:width_state, :] = state[...].astype(bf16)
        place = lax.broadcasted_iota(jnp.int32, (16, channels), 0)
        first = reached.astype(bf16).astype(f32)
        second = (reached - first).astype(bf16).astype(f32)
        third = reached - first - second
        parts = jnp.where(place == 0, first, jnp.where(place == 1, second, third))
        final_ref[width_state:, :] = parts.astype(bf16)


def scan(z, tokens, edge, slots, distances, middle, part, found, taps, skip, head, experts, depth, width, length):
    maps_all, cols, rows = found
    count, channels = tokens.shape[0], taps.shape[1]
    width_state = maps_all.shape[1] // 2
    far_distances = tuple(range(2, 2 + len(middle)))
    flat = [array for pair in middle for array in pair]
    block = lambda *shape: pl.BlockSpec(shape, lambda b, _: (b, 0))
    depth_rows = width // depth

    def columns_of(distance):
        return pl.BlockSpec(
            (length, depth_rows), lambda b, at: (b, lax.rem(at[0] - distance + depth, depth))
        )

    final_shape = (width_state + 16, channels)
    return pl.pallas_call(
        functools.partial(scan_kernel, head, experts, depth, width, distances, far_distances),
        grid_spec=pltpu.PrefetchScalarGridSpec(
            num_scalar_prefetch=1,
            grid=(count // length,),
            in_specs=[pl.BlockSpec(memory_space=pl.ANY)] * (len(slots) + len(flat))
            + [columns_of(distance) for distance in far_distances]
            + [
                pl.BlockSpec((length, extra), lambda b, _: (b, width // extra)),
                vmem(*edge.shape),
                block(length, part.shape[1]),
                block(length, maps_all.shape[1]),
                block(length, 128),
                pl.BlockSpec((rows.shape[0], length), lambda b, _: (0, b)),
                vmem(*taps.shape),
                vmem(*skip.shape),
            ],
            out_specs=[
                block(length, channels),
                block(length, channels),
                pl.BlockSpec(final_shape, lambda b, _: (0, 0)),
            ],
            scratch_shapes=[
                pltpu.VMEM((len(slots),) + slots[0].shape, bf16),
                pltpu.VMEM((len(middle),) + slots[0].shape, bf16),
                pltpu.VMEM((8 + length, channels), f32),
                pltpu.VMEM((width_state, channels), f32),
                pltpu.SemaphoreType.DMA((len(slots) + len(middle),)),
            ],
        ),
        out_shape=[
            jax.ShapeDtypeStruct((count, channels), f32),
            jax.ShapeDtypeStruct((count, channels), bf16),
            jax.ShapeDtypeStruct(final_shape, bf16),
        ],
        compiler_params=params(40),
        name="scan",
    )(z, *slots, *flat, *[tokens] * len(far_distances), tokens, edge, part, maps_all, cols, rows, taps, skip)


def norm_kernel(chunks, before, head, heads, pos_ref, maps_ref, cols_ref, gain_ref, *refs):
    ys, gates, finals = refs[:chunks], refs[chunks : 2 * chunks], refs[2 * chunks : 2 * chunks + before]
    theirs_ref, mine_ref, entering = refs[2 * chunks + before :]
    width_state = maps_ref.shape[1] // 2
    channels = mine_ref.shape[1]
    step, steps = pl.program_id(0), pl.num_programs(0)

    @pl.when(step == 0)
    def _():
        total = jnp.zeros((width_state, channels), f32)
        logs = jnp.zeros((1, channels), f32)
        for ref in finals:
            total = total + jnp.exp(logs) * ref[:width_state, :].astype(f32)
            parts = ref[width_state:, :].astype(f32)
            logs = logs + (parts[0:1] + parts[1:2] + parts[2:3])
        entering[...] = total.astype(bf16)

    lane = lax.broadcasted_iota(jnp.int32, (1, channels), 1)
    growth = 0.0
    for j in range(heads):
        reach = cols_ref[:, reach_lane + j : reach_lane + j + 1]
        growth = jnp.where(lane // head == j, jnp.exp(reach), growth)
    queries = maps_ref[:, width_state:]
    carried = growth * jnp.dot(queries, entering[...], preferred_element_type=f32)
    join = lambda parts: parts[0][...] if chunks == 1 else jnp.concatenate([p[...] for p in parts], axis=1)
    gate = join(gates).astype(f32)
    gated = (join(ys) + carried) * (gate / (1.0 + jnp.exp(-gate)))
    row = lax.broadcasted_iota(jnp.int32, (channels, channels), 0) // head
    col = lax.broadcasted_iota(jnp.int32, (channels, channels), 1) // head
    same = (row == col).astype(bf16)
    squares = gated * gated
    first = squares.astype(bf16)
    second = (squares - first.astype(f32)).astype(bf16)
    square = jnp.dot(first, same, preferred_element_type=f32) + jnp.dot(second, same, preferred_element_type=f32)
    square = square * (1.0 / head)
    normed = (gated * lax.rsqrt(square + 1e-05) * gain_ref[...]).astype(bf16)

    @pl.when(step < steps // 2)
    def _():
        theirs_ref[...] = normed

    @pl.when(step >= steps // 2)
    def _():
        mine_ref[...] = normed


def norm(core, found, gain, ys, gates, finals, head, length):
    maps_all, cols, _ = found
    count, channels = maps_all.shape[0] // 2, gain.shape[1]
    chunks, before = len(ys), len(finals)
    steps = count // length
    at = lambda b, core: (jnp.where(b < steps, 1 - core[0], core[0]) * steps + lax.rem(b, steps), 0)
    block = lambda *shape: pl.BlockSpec(shape, at)
    return pl.pallas_call(
        functools.partial(norm_kernel, chunks, before, head, channels // head),
        grid_spec=pltpu.PrefetchScalarGridSpec(
            num_scalar_prefetch=1,
            grid=(2 * steps,),
            in_specs=[block(length, maps_all.shape[1]), block(length, 128), vmem(*gain.shape)]
            + [block(length, channels // chunks)] * (2 * chunks)
            + [vmem(*array.shape) for array in finals],
            out_specs=[
                pl.BlockSpec((length, channels), lambda b, _: (jnp.minimum(b, steps - 1), 0)),
                pl.BlockSpec((length, channels), lambda b, _: (jnp.maximum(b - steps, 0), 0)),
            ],
            scratch_shapes=[pltpu.VMEM((maps_all.shape[1] // 2, channels), bf16)],
        ),
        out_shape=[jax.ShapeDtypeStruct((count, channels), bf16)] * 2,
        compiler_params=params(32),
        name="norm",
    )(core, maps_all, cols, gain, *ys, *gates, *finals)


def out_kernel(experts, groups, pos_ref, ids_ref, mine_ref, other_ref, *refs):
    weights, outs = refs[:-groups], refs[-groups:]
    group, width = pos_ref[0], mine_ref.shape[0] // groups
    chunk = weights[0].shape[1]
    for s in range(groups):
        rows = pl.ds(pl.multiple_of(jnp.bitwise_xor(group, s) * width, 64), width)
        chosen = ids_ref[rows, :].astype(f32)[:, 0:1]
        mine, other = mine_ref[rows, :], other_ref[rows, :]
        second = pos_ref[1] == 1
        both_halves = jnp.concatenate([jnp.where(second, other, mine), jnp.where(second, mine, other)], axis=1)
        zero = jnp.zeros_like(both_halves)
        masked = jnp.concatenate([jnp.where(chosen == e, both_halves, zero) for e in range(experts)], axis=1)
        for at, weight in enumerate(weights):
            total = jnp.dot(masked, weight[...], preferred_element_type=f32)
            outs[s][:, at * chunk : (at + 1) * chunk] = total.astype(bf16)


def project_out(position, ids, mine, other, weights, groups):
    rows = mine.shape[0] // groups
    whole = pl.BlockSpec(memory_space=pltpu.VMEM)
    shape = jax.ShapeDtypeStruct((rows, len(weights) * weights[0].shape[1]), bf16)
    return pl.pallas_call(
        functools.partial(out_kernel, groups // 2, groups),
        in_specs=[pl.BlockSpec(memory_space=pltpu.SMEM)] + [whole] * (3 + len(weights)),
        out_specs=[whole] * groups,
        out_shape=[shape] * groups,
        compiler_params=params(48),
        name="project_out",
    )(position, ids, mine, other, *weights)


def sum_kernel(depth, groups, distances, pos_ref, *refs):
    out_ref = refs[-1]
    chunk = out_ref.shape[1] // (2 * depth)
    for at, several in enumerate(distances):
        blocks = refs[at * groups : (at + 1) * groups]
        total = blocks[0][...].astype(f32)
        for block in blocks[1:]:
            total = total + block[...].astype(f32)
        total = total.astype(bf16)
        for place, distance in enumerate(several):
            z = lax.rem(pos_ref[0] - distance + depth, depth)
            for j in range(2):
                core = pos_ref[1] if j == 0 else 1 - pos_ref[1]
                to = pl.multiple_of((2 * z + core) * chunk, 128)
                span = slice((2 * place + j) * chunk, (2 * place + j + 1) * chunk)
                out_ref[:, pl.ds(to, chunk)] = total[:, span]


def add_up(position, blocks, distances, depth, width):
    groups, rows = len(blocks[0]), blocks[0][0].shape[0]
    flat = [block for several in blocks for block in several]
    whole = pl.BlockSpec(memory_space=pltpu.VMEM)
    return pl.pallas_call(
        functools.partial(sum_kernel, depth, groups, distances),
        in_specs=[pl.BlockSpec(memory_space=pltpu.SMEM)] + [whole] * len(flat),
        out_specs=whole,
        out_shape=jax.ShapeDtypeStruct((rows, width), bf16),
        compiler_params=params(48),
        name="add_up",
    )(position, *flat)


def spread_pieces(sent):
    return [
        shift(block, lambda z, k, e: (z, e % 2, (2 * (e // 2) + k) ^ r)) for r, block in enumerate(sent)
    ]


def arrange_kernel(blocks, by_rows, pos_ref, *refs):
    outs = refs[blocks:]
    for r, ref in enumerate(refs[:blocks]):
        to = jnp.bitwise_xor(pos_ref[0], r)
        for at, out in enumerate(outs):
            if by_rows:
                out[to] = ref[at * out.shape[1] : (at + 1) * out.shape[1], :]
                continue
            channels = out.shape[2] // 2
            for j in range(2):
                first = (j * len(outs) + at) * channels
                out[to, :, j * channels : (j + 1) * channels] = ref[:, first : first + channels]


def arrange(blocks, group, parts, by_rows):
    whole = pl.BlockSpec(memory_space=pltpu.VMEM)
    rows, width = blocks[0].shape
    shape = (len(blocks), rows // parts, width) if by_rows else (len(blocks), rows, width // parts)
    return pl.pallas_call(
        functools.partial(arrange_kernel, len(blocks), by_rows),
        in_specs=[pl.BlockSpec(memory_space=pltpu.SMEM)] + [whole] * len(blocks),
        out_specs=[whole] * parts,
        out_shape=[jax.ShapeDtypeStruct(shape, blocks[0].dtype)] * parts,
        compiler_params=params(32),
        name="arrange",
    )(group, *blocks)


def cut_rows_kernel(sources, pos_ref, *refs):
    for r, out in enumerate(refs[sources:]):
        piece = out.shape[0] // sources
        rows = pl.ds(pl.multiple_of(jnp.bitwise_xor(pos_ref[0], r) * piece, 64), piece)
        for at, ref in enumerate(refs[:sources]):
            out[at * piece : (at + 1) * piece, :] = ref[rows, :]


def cut_rows(group, arrays, groups):
    whole = pl.BlockSpec(memory_space=pltpu.VMEM)
    rows, width = arrays[0].shape
    shape = (len(arrays) * rows // groups, width)
    return pl.pallas_call(
        functools.partial(cut_rows_kernel, len(arrays)),
        in_specs=[pl.BlockSpec(memory_space=pltpu.SMEM)] + [whole] * len(arrays),
        out_specs=[whole] * groups,
        out_shape=[jax.ShapeDtypeStruct(shape, arrays[0].dtype)] * groups,
        compiler_params=params(32),
        name="cut_rows",
    )(group, *arrays)


def cut_kernel(pos_ref, flat_ref, *outs):
    piece = outs[0].shape[1] // 2
    half = flat_ref.shape[1] // 2
    for r, out in enumerate(outs):
        for j in range(2):
            at = pl.multiple_of(j * half + jnp.bitwise_xor(pos_ref[0], r) * piece, 128)
            out[:, j * piece : (j + 1) * piece] = flat_ref[:, pl.ds(at, piece)]


def cut(index, flat, groups):
    rows, half = flat.shape[0], flat.shape[1] // 2
    piece = half // groups
    if piece % 128:
        at = lambda j, r: j * half + jnp.bitwise_xor(index[0], r) * piece
        return [
            jnp.concatenate([lax.dynamic_slice(flat, (0, at(j, r)), (rows, piece)) for j in range(2)], axis=1)
            for r in range(groups)
        ]
    whole = pl.BlockSpec(memory_space=pltpu.VMEM)
    return pl.pallas_call(
        cut_kernel,
        in_specs=[pl.BlockSpec(memory_space=pltpu.SMEM), whole],
        out_specs=[whole] * groups,
        out_shape=[jax.ShapeDtypeStruct((rows, 2 * piece), flat.dtype)] * groups,
        compiler_params=params(32),
        name="cut",
    )(index, flat)


def lay_kernel(pos_ref, *refs):
    blocks, whole, sems = refs[:-2], refs[-2], refs[-1]
    rows = blocks[0].shape[0]
    copies = []
    for at, block in enumerate(blocks):
        row = pl.multiple_of(jnp.bitwise_xor(pos_ref[0], at) * rows, 64)
        copies.append(pltpu.make_async_copy(block, whole.at[pl.ds(row, rows), :], sems.at[at]))
    for copy in copies:
        copy.start()
    for copy in copies:
        copy.wait()


def lay(position, blocks):
    rows, width = blocks[0].shape
    place = pl.BlockSpec(memory_space=pl.ANY)
    return pl.pallas_call(
        lay_kernel,
        in_specs=[pl.BlockSpec(memory_space=pltpu.SMEM)] + [place] * len(blocks),
        out_specs=place,
        out_shape=jax.ShapeDtypeStruct((len(blocks) * rows, width), blocks[0].dtype),
        scratch_shapes=[pltpu.SemaphoreType.DMA((len(blocks),))],
        compiler_params=params(16),
        name="lay",
    )(position, *blocks)


def on_device(
    tokens, expert_ids, damping, in_weight, out_weight, w_bc, w_dt, rate, dt_bias, d_skip, gain, conv_weight
):
    groups, parts = lax.axis_size("exp"), lax.axis_size("ctx")
    depth, experts = parts // 2, groups // 2
    group, core, z = lax.axis_index("exp"), lax.axis_index("ctx") % 2, lax.axis_index("ctx") // 2
    rows, width = tokens.shape
    half = in_weight.shape[3]
    piece = half // groups
    heads = rate.shape[0] // 2
    head = piece // heads
    count = 2 * groups * rows
    length = 256 if count % 512 == 0 else 128
    scalar = lambda v: jnp.reshape(v, (1,)).astype(jnp.int32)
    z_at, group_at, core_at = scalar(z), scalar(group), scalar(core)
    depth_weight = in_weight.shape[1]
    swap = lambda array: shift(array, lambda z, k, e: (z, 1 - k, e))
    phase = lax.optimization_barrier

    flat = in_weight[0].reshape(depth_weight, 2 * half)
    index = scalar(2 * (group // 2) + core)
    got = spread_pieces(cut(index, flat, groups))
    out_raw = [out_weight[0], shift(out_weight[0], lambda z, k, e: ((z - 1) % depth, k, e))]
    added = jnp.concatenate(
        [expert_ids.astype(bf16), damping[:, None], jnp.zeros((rows, extra - 2), bf16)], axis=1
    )
    wide = jnp.concatenate([tokens, added], axis=1)
    got, wide, out_raw, w_bc, w_dt, rate, dt_bias, d_skip, gain, conv_weight = phase(
        (got, wide, out_raw, w_bc, w_dt, rate, dt_bias, d_skip, gain, conv_weight)
    )

    (shard,) = arrange(got, group_at, 1, False)
    shard = shard.reshape(groups * depth_weight, 2 * piece)
    near = line_near(shard, depth)
    wide, out_raw = phase((wide, out_raw, shard))[:2]
    exchange = lambda array, r: shift(array, lambda z, k, e: (z, k, e ^ r))
    own = [wide] + [exchange(wide, r) for r in range(1, groups)]
    local = lambda vector: lax.dynamic_slice_in_dim(vector, core * heads, heads, 0)
    lanes = lambda vector: jnp.concatenate(
        [jnp.pad(local(vector), (0, dt_lane - heads))] * (128 // dt_lane)
    )[None, :]
    picked = lax.dynamic_slice_in_dim(w_dt, (2 * group + core) * heads, heads, 0)
    picked = jnp.concatenate([jnp.pad(picked, ((0, dt_lane - heads), (0, 0)))] * (128 // dt_lane), axis=0)
    w_maps = jnp.concatenate([w_bc, picked.T], axis=1)
    bias_lanes, rate_lanes = lanes(dt_bias), lanes(rate)
    half_taps = lax.dynamic_slice_in_dim(conv_weight, core * piece, piece, 1)
    half_gain = lax.dynamic_slice_in_dim(gain, core * piece, piece, 0)[None, :]
    half_skip = jnp.repeat(local(d_skip), head)[None, :]
    out_sent = cut_rows(group_at, out_raw, groups)
    out_got = [out_sent[0]]
    for r in range(1, groups):
        own[r], block = phase((own[r], out_sent[r]))
        out_got.append(exchange(block, r))
    columns = out_weight.shape[2]
    part = lay(group_at, own)
    out_shard, above = [array.reshape(half, columns) for array in arrange(out_got, group_at, 2, True)]
    shard, near, part, out_shard, above, w_maps, bias_lanes, rate_lanes, half_taps, half_gain, half_skip = phase(
        (shard, near, part, out_shard, above, w_maps, bias_lanes, rate_lanes, half_taps, half_gain, half_skip)
    )

    far = line_far(near, depth)
    other_part = swap(part)
    plane = lay(core_at, [part, other_part])
    edge = shift(plane[count - halo :], lambda z, k, e: (z + 1, k, e) if z + 1 < depth else None)
    ids = lax.dynamic_slice(plane, (core * groups * rows, width), (groups * rows, extra))
    slots, distances = [shard, *near], (0, 1, depth - 1)
    part, *found = ahead(
        z_at, plane, w_maps, bias_lanes, rate_lanes, slots, distances, experts, depth, w_bc.shape[1], length
    )
    out_shard, above, _ = phase((out_shard, above, other_part))
    out_shard_other, above_other = swap(out_shard), swap(above)
    far, plane, edge, found, part, ids, out_shard, above, out_shard_other, above_other = phase(
        (far, plane, edge, found, part, ids, out_shard, above, out_shard_other, above_other)
    )

    y, gate, final = scan(
        z_at, plane, edge, slots, distances, far, part, found, half_taps, half_skip,
        head, experts, depth, width, length,
    )
    below = shift(out_shard, lambda z, k, e: ((z + 1) % depth, k, e))
    y, gate, final, below = phase((y, gate, final, below))

    finals = [
        shift(final, lambda z, k, e: (z + s, k, e) if z + s < depth else None) for s in range(1, depth)
    ]
    ups, downs = [below], [above]
    for s in range(2, depth - 1):
        ups.append(step_up(ups[-1], s, depth))
        downs.append(step_down(downs[-1], s, depth))
    theirs, mine = norm(core_at, found, half_gain, [y], [gate], finals, head, length)
    theirs, mine, below = phase((theirs, mine, below))
    other = swap(theirs)
    below_other = swap(below)
    other, mine = phase((other, mine))

    position = jnp.concatenate([group_at, core_at])

    def send(*weights):
        results = project_out(position, ids, mine, other, weights, groups)
        return [results[0]] + [exchange(results[r], r) for r in range(1, groups)]

    blocks = [send(out_shard, out_shard_other, above, above_other)]
    ups, downs, below_other, blocks[0][0] = phase((ups, downs, below_other, blocks[0][0]))
    late = [jnp.where(z >= s + 2, up, down) for s, (up, down) in enumerate(paired(ups[1:], downs[1:]))]
    def swap_in_parts(array):
        rows_each = array.shape[0] // 2
        return jnp.concatenate(
            [swap(array[i * rows_each : (i + 1) * rows_each]) for i in range(2)], axis=0
        )

    blocks.append(send(below, below_other, *[array for part in late for array in (part, swap_in_parts(part))]))
    order = [(0, depth - 1), (1, *range(2, depth - 1))]
    return add_up(jnp.concatenate([z_at, core_at]), blocks, order, depth, width)


def solution(mesh):
    placed = (
        P(("ctx", "exp"), None),
        P(("ctx", "exp"), None),
        P(("ctx", "exp")),
        P("exp", "ctx", None, None),
        P("exp", None, "ctx"),
        P(),
        P(),
        P("exp"),
        P("exp"),
        P("exp"),
        P("exp"),
        P(None, "exp"),
    )
    return jax.shard_map(
        on_device, mesh=mesh, in_specs=placed, out_specs=P(("ctx", "exp"), None), check_vma=False
    )
```

```python
import functools

import jax
import jax.numpy as jnp
from jax import lax
from jax.experimental import pallas as pl
from jax.experimental.pallas import tpu as pltpu
from jax.sharding import PartitionSpec as P

both = ("ctx", "exp")
extra = 128
halo = 16
dt_lane, reach_lane = 16, 32
highest = lax.Precision.HIGHEST
f32, bf16 = jnp.float32, jnp.bfloat16


def params(mib):
    return pltpu.CompilerParams(vmem_limit_bytes=mib << 20)


def vmem(*shape):
    return pl.BlockSpec(shape, lambda *_: (0,) * len(shape), pipeline_mode=pl.Buffered(1))


def shift(array, move):
    groups = lax.axis_size("exp")
    pairs = []
    for c in range(lax.axis_size("ctx")):
        for e in range(groups):
            to = move(c // 2, c % 2, e)
            if to is not None:
                pairs.append((c * groups + e, (2 * to[0] + to[1]) * groups + to[2]))
    return lax.ppermute(array, both, pairs)


def line_near(own, depth):
    return (
        shift(own, lambda z, k, e: ((z + 1) % depth, k, e)),
        shift(own, lambda z, k, e: ((z - 1) % depth, k, e)),
    )


def step_up(array, s, depth):
    return shift(array, lambda z, k, e: (z + 1, k, e) if s - 1 <= z < depth - 1 else None)


def step_down(array, s, depth):
    return shift(array, lambda z, k, e: (z - 1, k, e) if 0 < z <= depth - s else None)


def line_far(near, depth):
    ups, downs = [], []
    up, down = near
    for s in range(2, depth - 1):
        up, down = step_up(up, s, depth), step_down(down, s, depth)
        ups.append(up)
        downs.append(down)
    return paired(ups, downs)


def paired(ups, downs):
    return list(zip(ups, downs[::-1]))


def slice_of(z, distance, depth, rows):
    return pl.multiple_of(lax.rem(z - distance + depth, depth) * rows, 128)


def choose(extra_lanes, parts):
    chosen = extra_lanes.astype(f32)[:, 0:1]
    total = parts[0]
    for e in range(1, len(parts)):
        total = jnp.where(chosen == e, parts[e], total)
    return total


def ahead_kernel(experts, depth, width, distances, pos_ref, x_ref, w_ref, bias_ref, rate_ref, *refs):
    slots, (part_ref, maps_ref, cols_ref, rows_ref, total) = refs[: len(distances)], refs[len(distances) :]
    length = x_ref.shape[0]

    @pl.when(pl.program_id(0) == 0)
    def _():
        total[...] = jnp.zeros_like(total)

    added = x_ref[:, width:]
    found = jnp.dot(x_ref[:, :width], w_ref[...], preferred_element_type=f32).astype(bf16)
    state2 = maps_ref.shape[1]
    maps_ref[...] = found[:, :state2]
    raw = found[:, state2:].astype(f32) + bias_ref[...]
    steps = jnp.maximum(raw, 0.0) + jnp.log1p(jnp.exp(-jnp.abs(raw)))
    logs = -(rate_ref[...] * steps + added.astype(f32)[:, 1:2])
    first = logs.astype(bf16)
    second = (logs - first.astype(f32)).astype(bf16)
    third = (logs - first.astype(f32) - second.astype(f32)).astype(bf16)
    row = lax.broadcasted_iota(jnp.int32, (length, length), 0)
    col = lax.broadcasted_iota(jnp.int32, (length, length), 1)
    lower = (row >= col).astype(bf16)
    sums = jnp.dot(lower, jnp.concatenate([first, second, third], axis=1), preferred_element_type=f32)
    climb = sums[:, :128] + (sums[:, 128:256] + sums[:, 256:])
    lane = lax.broadcasted_iota(jnp.int32, climb.shape, 1)
    reach = climb + total[...]
    packed = jnp.where(lane < dt_lane, climb, jnp.where(lane < reach_lane, steps, reach))
    cols_ref[...] = packed
    rows_ref[...] = jnp.transpose(packed)[: rows_ref.shape[0]]
    total[...] = reach[length - 1 : length]

    depth_rows = width // depth
    parts = []
    for e in range(experts):
        part = 0.0
        for distance, slot in zip(distances, slots):
            x = x_ref[:, pl.ds(slice_of(pos_ref[0], distance, depth, depth_rows), depth_rows)]
            part += jnp.dot(x, slot[e * depth_rows : (e + 1) * depth_rows, :], preferred_element_type=f32)
        parts.append(part)
    part_ref[...] = choose(added, parts)


def ahead(position, tokens, w_maps, bias, rate, slots, distances, experts, depth, state2, length):
    count, width, columns = tokens.shape[0], w_maps.shape[0], slots[0].shape[1]
    block = lambda *shape: pl.BlockSpec(shape, lambda b, _: (b, 0))
    return pl.pallas_call(
        functools.partial(ahead_kernel, experts, depth, width, distances),
        grid_spec=pltpu.PrefetchScalarGridSpec(
            num_scalar_prefetch=1,
            grid=(count // length,),
            in_specs=[block(length, tokens.shape[1])]
            + [vmem(*w_maps.shape), vmem(1, 128), vmem(1, 128)]
            + [vmem(*slot.shape) for slot in slots],
            out_specs=[
                block(length, columns),
                block(length, state2),
                block(length, 128),
                pl.BlockSpec((reach_lane, length), lambda b, _: (0, b)),
            ],
            scratch_shapes=[pltpu.VMEM((1, 128), f32)],
        ),
        out_shape=[
            jax.ShapeDtypeStruct((count, columns), f32),
            jax.ShapeDtypeStruct((count, state2), bf16),
            jax.ShapeDtypeStruct((count, 128), f32),
            jax.ShapeDtypeStruct((reach_lane, count), f32),
        ],
        compiler_params=params(40),
        name="ahead",
    )(position, tokens, w_maps, bias, rate, *slots)


def scan_kernel(head, experts, depth, width, distances, middle, pos_ref, *refs):
    near, count = len(distances), len(middle)
    slots, pairs = refs[:near], refs[near : near + 2 * count]
    xs, refs = refs[near + 2 * count : near + 3 * count], refs[near + 3 * count :]
    extra_ref, edge_ref, part_ref, maps_ref, cols_ref, rows_ref, taps_ref, skip_ref = refs[:8]
    y_ref, gate_ref, final_ref, nears, fars, seen, state, sems = refs[8:]
    length, channels = y_ref.shape
    taps = taps_ref.shape[0]
    width_state = maps_ref.shape[1] // 2
    step, z = pl.program_id(0), pos_ref[0]
    depth_rows = width // depth
    near_copies = [pltpu.make_async_copy(slots[i], nears.at[i], sems.at[i]) for i in range(near)]

    def far(m, action):
        up, down = (
            pltpu.make_async_copy(pairs[2 * m + i], fars.at[m], sems.at[near + m]) for i in range(2)
        )

        @pl.when(z >= middle[m])
        def _():
            action(up)

        @pl.when(z < middle[m])
        def _():
            action(down)

    def expert(ref, e):
        return ref[e * depth_rows : (e + 1) * depth_rows, :]

    @pl.when(step == 0)
    def _():
        for m in range(count):
            far(m, lambda copy: copy.start())
        for copy in near_copies:
            copy.start()
        state[...] = jnp.zeros_like(state)
        for m in range(count):
            far(m, lambda copy: copy.wait())
        for copy in near_copies:
            copy.wait()
        parts = []
        for e in range(experts):
            total = 0.0
            for distance, ref in [(d, nears.at[i]) for i, d in enumerate(distances)] + [
                (d, fars.at[i]) for i, d in enumerate(middle)
            ]:
                x = edge_ref[:, pl.ds(slice_of(z, distance, depth, depth_rows), depth_rows)]
                total += jnp.dot(x, expert(ref, e), preferred_element_type=f32)
            parts.append(total)
        before = choose(edge_ref[:, width:], parts).astype(bf16).astype(f32)
        seen[0:8, :] = before[halo - 8 :, :channels]

    parts = []
    for e in range(experts):
        total = 0.0
        for m in range(count):
            total += jnp.dot(xs[m][...], expert(fars.at[m], e), preferred_element_type=f32)
        parts.append(total)
    whole = (part_ref[...] + choose(extra_ref[...], parts)).astype(bf16)
    gate_ref[...] = whole[:, channels:]
    seen[8:, :] = whole[:, :channels].astype(f32)
    mixed = jnp.zeros((length, channels), f32)
    for tap in range(taps):
        mixed = mixed + taps_ref[tap : tap + 1, :] * seen[pl.ds(8 - (taps - 1) + tap, length), :]
    seen[0:8, :] = seen[pl.ds(length, 8), :]
    values = mixed / (1.0 + jnp.exp(-mixed))

    keys, queries = maps_ref[:, :width_state], maps_ref[:, width_state:]
    gram = lax.dot_general(queries, keys, (((1,), (1,)), ((), ())), preferred_element_type=f32)
    row = lax.broadcasted_iota(jnp.int32, (length, length), 0)
    col = lax.broadcasted_iota(jnp.int32, (length, length), 1)
    lower = row >= col
    gram = jnp.where(lower, gram, 0.0)
    lane = lax.broadcasted_iota(jnp.int32, (1, channels), 1)
    rounded = values.astype(bf16)
    inside, growth, ends, decay, reached = [], 0.0, 0.0, 0.0, 0.0
    for j in range(channels // head):
        mine = lane // head == j
        climb, size = cols_ref[:, j : j + 1], cols_ref[:, dt_lane + j : dt_lane + j + 1]
        climb_row, size_row = rows_ref[j : j + 1, :], rows_ref[dt_lane + j : dt_lane + j + 1, :]
        spread = jnp.exp(jnp.where(lower, climb - climb_row, 0.0)) * gram * size_row
        inside.append(
            jnp.dot(
                spread.astype(bf16), rounded[:, j * head : (j + 1) * head], preferred_element_type=f32
            )
        )
        last = climb[length - 1 : length]
        growth = jnp.where(mine, jnp.exp(climb), growth)
        ends = jnp.where(mine, jnp.exp(last - climb) * size, ends)
        decay = jnp.where(mine, jnp.exp(last), decay)
        reach = cols_ref[length - 1 : length, reach_lane + j : reach_lane + j + 1]
        reached = jnp.where(mine, reach, reached)
    inside = inside[0] if len(inside) == 1 else jnp.concatenate(inside, axis=1)
    carried = jnp.dot(queries, state[...].astype(bf16), preferred_element_type=f32)
    y_ref[...] = inside + growth * carried + skip_ref[...] * values
    fresh = lax.dot_general(
        keys, (ends * values).astype(bf16), (((0,), (0,)), ((), ())), preferred_element_type=f32
    )
    state[...] = decay * state[...] + fresh

    @pl.when(step == pl.num_programs(0) - 1)
    def _():
        final_ref[:width_state, :] = state[...].astype(bf16)
        place = lax.broadcasted_iota(jnp.int32, (16, channels), 0)
        first = reached.astype(bf16).astype(f32)
        second = (reached - first).astype(bf16).astype(f32)
        third = reached - first - second
        parts = jnp.where(place == 0, first, jnp.where(place == 1, second, third))
        final_ref[width_state:, :] = parts.astype(bf16)


def scan(z, tokens, edge, slots, distances, middle, part, found, taps, skip, head, experts, depth, width, length):
    maps_all, cols, rows = found
    count, channels = tokens.shape[0], taps.shape[1]
    width_state = maps_all.shape[1] // 2
    far_distances = tuple(range(2, 2 + len(middle)))
    flat = [array for pair in middle for array in pair]
    block = lambda *shape: pl.BlockSpec(shape, lambda b, _: (b, 0))
    depth_rows = width // depth

    def columns_of(distance):
        return pl.BlockSpec(
            (length, depth_rows), lambda b, at: (b, lax.rem(at[0] - distance + depth, depth))
        )

    final_shape = (width_state + 16, channels)
    return pl.pallas_call(
        functools.partial(scan_kernel, head, experts, depth, width, distances, far_distances),
        grid_spec=pltpu.PrefetchScalarGridSpec(
            num_scalar_prefetch=1,
            grid=(count // length,),
            in_specs=[pl.BlockSpec(memory_space=pl.ANY)] * (len(slots) + len(flat))
            + [columns_of(distance) for distance in far_distances]
            + [
                pl.BlockSpec((length, extra), lambda b, _: (b, width // extra)),
                vmem(*edge.shape),
                block(length, part.shape[1]),
                block(length, maps_all.shape[1]),
                block(length, 128),
                pl.BlockSpec((rows.shape[0], length), lambda b, _: (0, b)),
                vmem(*taps.shape),
                vmem(*skip.shape),
            ],
            out_specs=[
                block(length, channels),
                block(length, channels),
                pl.BlockSpec(final_shape, lambda b, _: (0, 0)),
            ],
            scratch_shapes=[
                pltpu.VMEM((len(slots),) + slots[0].shape, bf16),
                pltpu.VMEM((len(middle),) + slots[0].shape, bf16),
                pltpu.VMEM((8 + length, channels), f32),
                pltpu.VMEM((width_state, channels), f32),
                pltpu.SemaphoreType.DMA((len(slots) + len(middle),)),
            ],
        ),
        out_shape=[
            jax.ShapeDtypeStruct((count, channels), f32),
            jax.ShapeDtypeStruct((count, channels), bf16),
            jax.ShapeDtypeStruct(final_shape, bf16),
        ],
        compiler_params=params(40),
        name="scan",
    )(z, *slots, *flat, *[tokens] * len(far_distances), tokens, edge, part, maps_all, cols, rows, taps, skip)


def norm_kernel(chunks, before, head, heads, pos_ref, maps_ref, cols_ref, gain_ref, *refs):
    ys, gates, finals = refs[:chunks], refs[chunks : 2 * chunks], refs[2 * chunks : 2 * chunks + before]
    theirs_ref, mine_ref, entering = refs[2 * chunks + before :]
    width_state = maps_ref.shape[1] // 2
    channels = mine_ref.shape[1]
    step, steps = pl.program_id(0), pl.num_programs(0)

    @pl.when(step == 0)
    def _():
        total = jnp.zeros((width_state, channels), f32)
        logs = jnp.zeros((1, channels), f32)
        for ref in finals:
            total = total + jnp.exp(logs) * ref[:width_state, :].astype(f32)
            parts = ref[width_state:, :].astype(f32)
            logs = logs + (parts[0:1] + parts[1:2] + parts[2:3])
        entering[...] = total.astype(bf16)

    lane = lax.broadcasted_iota(jnp.int32, (1, channels), 1)
    growth = 0.0
    for j in range(heads):
        reach = cols_ref[:, reach_lane + j : reach_lane + j + 1]
        growth = jnp.where(lane // head == j, jnp.exp(reach), growth)
    queries = maps_ref[:, width_state:]
    carried = growth * jnp.dot(queries, entering[...], preferred_element_type=f32)
    join = lambda parts: parts[0][...] if chunks == 1 else jnp.concatenate([p[...] for p in parts], axis=1)
    gate = join(gates).astype(f32)
    gated = (join(ys) + carried) * (gate / (1.0 + jnp.exp(-gate)))
    row = lax.broadcasted_iota(jnp.int32, (channels, channels), 0) // head
    col = lax.broadcasted_iota(jnp.int32, (channels, channels), 1) // head
    same = (row == col).astype(bf16)
    squares = gated * gated
    first = squares.astype(bf16)
    second = (squares - first.astype(f32)).astype(bf16)
    square = jnp.dot(first, same, preferred_element_type=f32) + jnp.dot(second, same, preferred_element_type=f32)
    square = square * (1.0 / head)
    normed = (gated * lax.rsqrt(square + 1e-05) * gain_ref[...]).astype(bf16)

    @pl.when(step < steps // 2)
    def _():
        theirs_ref[...] = normed

    @pl.when(step >= steps // 2)
    def _():
        mine_ref[...] = normed


def norm(core, found, gain, ys, gates, finals, head, length):
    maps_all, cols, _ = found
    count, channels = maps_all.shape[0] // 2, gain.shape[1]
    chunks, before = len(ys), len(finals)
    steps = count // length
    at = lambda b, core: (jnp.where(b < steps, 1 - core[0], core[0]) * steps + lax.rem(b, steps), 0)
    block = lambda *shape: pl.BlockSpec(shape, at)
    return pl.pallas_call(
        functools.partial(norm_kernel, chunks, before, head, channels // head),
        grid_spec=pltpu.PrefetchScalarGridSpec(
            num_scalar_prefetch=1,
            grid=(2 * steps,),
            in_specs=[block(length, maps_all.shape[1]), block(length, 128), vmem(*gain.shape)]
            + [block(length, channels // chunks)] * (2 * chunks)
            + [vmem(*array.shape) for array in finals],
            out_specs=[
                pl.BlockSpec((length, channels), lambda b, _: (jnp.minimum(b, steps - 1), 0)),
                pl.BlockSpec((length, channels), lambda b, _: (jnp.maximum(b - steps, 0), 0)),
            ],
            scratch_shapes=[pltpu.VMEM((maps_all.shape[1] // 2, channels), bf16)],
        ),
        out_shape=[jax.ShapeDtypeStruct((count, channels), bf16)] * 2,
        compiler_params=params(32),
        name="norm",
    )(core, maps_all, cols, gain, *ys, *gates, *finals)


def out_kernel(experts, groups, pos_ref, ids_ref, mine_ref, other_ref, *refs):
    weights, outs = refs[:-groups], refs[-groups:]
    group, width = pos_ref[0], mine_ref.shape[0] // groups
    chunk = weights[0].shape[1]
    for s in range(groups):
        rows = pl.ds(pl.multiple_of(jnp.bitwise_xor(group, s) * width, 64), width)
        chosen = ids_ref[rows, :].astype(f32)[:, 0:1]
        mine, other = mine_ref[rows, :], other_ref[rows, :]
        second = pos_ref[1] == 1
        both_halves = jnp.concatenate([jnp.where(second, other, mine), jnp.where(second, mine, other)], axis=1)
        zero = jnp.zeros_like(both_halves)
        masked = jnp.concatenate([jnp.where(chosen == e, both_halves, zero) for e in range(experts)], axis=1)
        for at, weight in enumerate(weights):
            total = jnp.dot(masked, weight[...], preferred_element_type=f32)
            outs[s][:, at * chunk : (at + 1) * chunk] = total.astype(bf16)


def project_out(position, ids, mine, other, weights, groups):
    rows = mine.shape[0] // groups
    whole = pl.BlockSpec(memory_space=pltpu.VMEM)
    shape = jax.ShapeDtypeStruct((rows, len(weights) * weights[0].shape[1]), bf16)
    return pl.pallas_call(
        functools.partial(out_kernel, groups // 2, groups),
        in_specs=[pl.BlockSpec(memory_space=pltpu.SMEM)] + [whole] * (3 + len(weights)),
        out_specs=[whole] * groups,
        out_shape=[shape] * groups,
        compiler_params=params(48),
        name="project_out",
    )(position, ids, mine, other, *weights)


def sum_kernel(depth, groups, distances, pos_ref, *refs):
    out_ref = refs[-1]
    chunk = out_ref.shape[1] // (2 * depth)
    for at, several in enumerate(distances):
        blocks = refs[at * groups : (at + 1) * groups]
        total = blocks[0][...].astype(f32)
        for block in blocks[1:]:
            total = total + block[...].astype(f32)
        total = total.astype(bf16)
        for place, distance in enumerate(several):
            z = lax.rem(pos_ref[0] - distance + depth, depth)
            for j in range(2):
                core = pos_ref[1] if j == 0 else 1 - pos_ref[1]
                to = pl.multiple_of((2 * z + core) * chunk, 128)
                span = slice((2 * place + j) * chunk, (2 * place + j + 1) * chunk)
                out_ref[:, pl.ds(to, chunk)] = total[:, span]


def add_up(position, blocks, distances, depth, width):
    groups, rows = len(blocks[0]), blocks[0][0].shape[0]
    flat = [block for several in blocks for block in several]
    whole = pl.BlockSpec(memory_space=pltpu.VMEM)
    return pl.pallas_call(
        functools.partial(sum_kernel, depth, groups, distances),
        in_specs=[pl.BlockSpec(memory_space=pltpu.SMEM)] + [whole] * len(flat),
        out_specs=whole,
        out_shape=jax.ShapeDtypeStruct((rows, width), bf16),
        compiler_params=params(48),
        name="add_up",
    )(position, *flat)


def spread_pieces(sent):
    return [
        shift(block, lambda z, k, e: (z, e % 2, (2 * (e // 2) + k) ^ r)) for r, block in enumerate(sent)
    ]


def arrange_kernel(blocks, by_rows, pos_ref, *refs):
    outs = refs[blocks:]
    for r, ref in enumerate(refs[:blocks]):
        to = jnp.bitwise_xor(pos_ref[0], r)
        for at, out in enumerate(outs):
            if by_rows:
                out[to] = ref[at * out.shape[1] : (at + 1) * out.shape[1], :]
                continue
            channels = out.shape[2] // 2
            for j in range(2):
                first = (j * len(outs) + at) * channels
                out[to, :, j * channels : (j + 1) * channels] = ref[:, first : first + channels]


def arrange(blocks, group, parts, by_rows):
    whole = pl.BlockSpec(memory_space=pltpu.VMEM)
    rows, width = blocks[0].shape
    shape = (len(blocks), rows // parts, width) if by_rows else (len(blocks), rows, width // parts)
    return pl.pallas_call(
        functools.partial(arrange_kernel, len(blocks), by_rows),
        in_specs=[pl.BlockSpec(memory_space=pltpu.SMEM)] + [whole] * len(blocks),
        out_specs=[whole] * parts,
        out_shape=[jax.ShapeDtypeStruct(shape, blocks[0].dtype)] * parts,
        compiler_params=params(32),
        name="arrange",
    )(group, *blocks)


def cut_rows_kernel(sources, pos_ref, *refs):
    for r, out in enumerate(refs[sources:]):
        piece = out.shape[0] // sources
        rows = pl.ds(pl.multiple_of(jnp.bitwise_xor(pos_ref[0], r) * piece, 64), piece)
        for at, ref in enumerate(refs[:sources]):
            out[at * piece : (at + 1) * piece, :] = ref[rows, :]


def cut_rows(group, arrays, groups):
    whole = pl.BlockSpec(memory_space=pltpu.VMEM)
    rows, width = arrays[0].shape
    shape = (len(arrays) * rows // groups, width)
    return pl.pallas_call(
        functools.partial(cut_rows_kernel, len(arrays)),
        in_specs=[pl.BlockSpec(memory_space=pltpu.SMEM)] + [whole] * len(arrays),
        out_specs=[whole] * groups,
        out_shape=[jax.ShapeDtypeStruct(shape, arrays[0].dtype)] * groups,
        compiler_params=params(32),
        name="cut_rows",
    )(group, *arrays)


def cut_kernel(pos_ref, flat_ref, *outs):
    piece = outs[0].shape[1] // 2
    half = flat_ref.shape[1] // 2
    for r, out in enumerate(outs):
        for j in range(2):
            at = pl.multiple_of(j * half + jnp.bitwise_xor(pos_ref[0], r) * piece, 128)
            out[:, j * piece : (j + 1) * piece] = flat_ref[:, pl.ds(at, piece)]


def cut(index, flat, groups):
    rows, half = flat.shape[0], flat.shape[1] // 2
    piece = half // groups
    if piece % 128:
        at = lambda j, r: j * half + jnp.bitwise_xor(index[0], r) * piece
        return [
            jnp.concatenate([lax.dynamic_slice(flat, (0, at(j, r)), (rows, piece)) for j in range(2)], axis=1)
            for r in range(groups)
        ]
    whole = pl.BlockSpec(memory_space=pltpu.VMEM)
    return pl.pallas_call(
        cut_kernel,
        in_specs=[pl.BlockSpec(memory_space=pltpu.SMEM), whole],
        out_specs=[whole] * groups,
        out_shape=[jax.ShapeDtypeStruct((rows, 2 * piece), flat.dtype)] * groups,
        compiler_params=params(32),
        name="cut",
    )(index, flat)


def lay_kernel(pos_ref, *refs):
    blocks, whole, sems = refs[:-2], refs[-2], refs[-1]
    rows = blocks[0].shape[0]
    copies = []
    for at, block in enumerate(blocks):
        row = pl.multiple_of(jnp.bitwise_xor(pos_ref[0], at) * rows, 64)
        copies.append(pltpu.make_async_copy(block, whole.at[pl.ds(row, rows), :], sems.at[at]))
    for copy in copies:
        copy.start()
    for copy in copies:
        copy.wait()


def lay(position, blocks):
    rows, width = blocks[0].shape
    place = pl.BlockSpec(memory_space=pl.ANY)
    return pl.pallas_call(
        lay_kernel,
        in_specs=[pl.BlockSpec(memory_space=pltpu.SMEM)] + [place] * len(blocks),
        out_specs=place,
        out_shape=jax.ShapeDtypeStruct((len(blocks) * rows, width), blocks[0].dtype),
        scratch_shapes=[pltpu.SemaphoreType.DMA((len(blocks),))],
        compiler_params=params(16),
        name="lay",
    )(position, *blocks)


def on_device(
    tokens, expert_ids, damping, in_weight, out_weight, w_bc, w_dt, rate, dt_bias, d_skip, gain, conv_weight
):
    groups, parts = lax.axis_size("exp"), lax.axis_size("ctx")
    depth, experts = parts // 2, groups // 2
    group, core, z = lax.axis_index("exp"), lax.axis_index("ctx") % 2, lax.axis_index("ctx") // 2
    rows, width = tokens.shape
    half = in_weight.shape[3]
    piece = half // groups
    heads = rate.shape[0] // 2
    head = piece // heads
    count = 2 * groups * rows
    length = 256 if count % 512 == 0 else 128
    scalar = lambda v: jnp.reshape(v, (1,)).astype(jnp.int32)
    z_at, group_at, core_at = scalar(z), scalar(group), scalar(core)
    depth_weight = in_weight.shape[1]
    swap = lambda array: shift(array, lambda z, k, e: (z, 1 - k, e))
    phase = lax.optimization_barrier

    flat = in_weight[0].reshape(depth_weight, 2 * half)
    index = scalar(2 * (group // 2) + core)
    got = spread_pieces(cut(index, flat, groups))
    out_raw = [out_weight[0], shift(out_weight[0], lambda z, k, e: ((z - 1) % depth, k, e))]
    added = jnp.concatenate(
        [expert_ids.astype(bf16), damping[:, None], jnp.zeros((rows, extra - 2), bf16)], axis=1
    )
    wide = jnp.concatenate([tokens, added], axis=1)
    got, wide, out_raw, w_bc, w_dt, rate, dt_bias, d_skip, gain, conv_weight = phase(
        (got, wide, out_raw, w_bc, w_dt, rate, dt_bias, d_skip, gain, conv_weight)
    )

    (shard,) = arrange(got, group_at, 1, False)
    shard = shard.reshape(groups * depth_weight, 2 * piece)
    near = line_near(shard, depth)
    wide, out_raw = phase((wide, out_raw, shard))[:2]
    exchange = lambda array, r: shift(array, lambda z, k, e: (z, k, e ^ r))
    own = [wide] + [exchange(wide, r) for r in range(groups - 1, 0, -1)][::-1]
    local = lambda vector: lax.dynamic_slice_in_dim(vector, core * heads, heads, 0)
    lanes = lambda vector: jnp.concatenate(
        [jnp.pad(local(vector), (0, dt_lane - heads))] * (128 // dt_lane)
    )[None, :]
    picked = lax.dynamic_slice_in_dim(w_dt, (2 * group + core) * heads, heads, 0)
    picked = jnp.concatenate([jnp.pad(picked, ((0, dt_lane - heads), (0, 0)))] * (128 // dt_lane), axis=0)
    w_maps = jnp.concatenate([w_bc, picked.T], axis=1)
    bias_lanes, rate_lanes = lanes(dt_bias), lanes(rate)
    half_taps = lax.dynamic_slice_in_dim(conv_weight, core * piece, piece, 1)
    half_gain = lax.dynamic_slice_in_dim(gain, core * piece, piece, 0)[None, :]
    half_skip = jnp.repeat(local(d_skip), head)[None, :]
    out_sent = cut_rows(group_at, out_raw, groups)
    out_got = [out_sent[0]]
    for r in range(1, groups):
        own[r], block = phase((own[r], out_sent[r]))
        out_got.append(exchange(block, r))
    columns = out_weight.shape[2]
    part = lay(group_at, own)
    out_shard, above = [array.reshape(half, columns) for array in arrange(out_got, group_at, 2, True)]
    shard, near, part, out_shard, above, w_maps, bias_lanes, rate_lanes, half_taps, half_gain, half_skip = phase(
        (shard, near, part, out_shard, above, w_maps, bias_lanes, rate_lanes, half_taps, half_gain, half_skip)
    )

    far = line_far(near, depth)
    other_part = swap(part)
    plane = lay(core_at, [part, other_part])
    edge = shift(plane[count - halo :], lambda z, k, e: (z + 1, k, e) if z + 1 < depth else None)
    ids = lax.dynamic_slice(plane, (core * groups * rows, width), (groups * rows, extra))
    slots, distances = [shard, *near], (0, 1, depth - 1)
    part, *found = ahead(
        z_at, plane, w_maps, bias_lanes, rate_lanes, slots, distances, experts, depth, w_bc.shape[1], length
    )
    out_shard, above, _ = phase((out_shard, above, other_part))
    out_shard_other, above_other = swap(out_shard), swap(above)
    far, plane, edge, found, part, ids, out_shard, above, out_shard_other, above_other = phase(
        (far, plane, edge, found, part, ids, out_shard, above, out_shard_other, above_other)
    )

    y, gate, final = scan(
        z_at, plane, edge, slots, distances, far, part, found, half_taps, half_skip,
        head, experts, depth, width, length,
    )
    below = shift(out_shard, lambda z, k, e: ((z + 1) % depth, k, e))
    downs = [above]
    for s in range(2, depth - 1):
        downs.append(step_down(downs[-1], s, depth))
    y, gate, final, below = phase((y, gate, final, below))

    finals = [
        shift(final, lambda z, k, e: (z + s, k, e) if z + s < depth else None) for s in range(1, depth)
    ]
    ups = [below]
    for s in range(2, depth - 1):
        ups.append(step_up(ups[-1], s, depth))
    theirs, mine = norm(core_at, found, half_gain, [y], [gate], finals, head, length)
    theirs, mine, below = phase((theirs, mine, below))
    other = swap(theirs)
    below_other = swap(below)
    other, mine = phase((other, mine))

    position = jnp.concatenate([group_at, core_at])

    def send(*weights):
        results = project_out(position, ids, mine, other, weights, groups)
        return [results[0]] + [exchange(results[r], r) for r in range(groups - 1, 0, -1)][::-1]

    blocks = [send(out_shard, out_shard_other, above, above_other)]
    ups, downs, below_other, blocks[0][0] = phase((ups, downs, below_other, blocks[0][0]))
    late = [jnp.where(z >= s + 2, up, down) for s, (up, down) in enumerate(paired(ups[1:], downs[1:]))]
    def swap_in_parts(array):
        rows_each = array.shape[0] // 2
        return jnp.concatenate(
            [swap(array[i * rows_each : (i + 1) * rows_each]) for i in range(2)], axis=0
        )

    blocks.append(send(below, below_other, *[array for part in late for array in (part, swap_in_parts(part))]))
    order = [(0, depth - 1), (1, *range(2, depth - 1))]
    return add_up(jnp.concatenate([z_at, core_at]), blocks, order, depth, width)


def solution(mesh):
    placed = (
        P(("ctx", "exp"), None),
        P(("ctx", "exp"), None),
        P(("ctx", "exp")),
        P("exp", "ctx", None, None),
        P("exp", None, "ctx"),
        P(),
        P(),
        P("exp"),
        P("exp"),
        P("exp"),
        P("exp"),
        P(None, "exp"),
    )
    return jax.shard_map(
        on_device, mesh=mesh, in_specs=placed, out_specs=P(("ctx", "exp"), None), check_vma=False
    )
```
